512 devices in a mesh: dom: 32 (over z, x), mode: 16 (over y, core).
Axes of the slice: x: 4, y: 8, z: 8, core: 2. Of those that a mesh axis runs over, the one named last changes fastest.
Arguments:
- shapes: bfloat16 [3, 8192, 4096], P(None, 'dom', 'mode'), may hold values from -6 to 6
- masses: float32 [8192], P('dom'), may hold values from 0.1 to 30, as said below
- spectral: float32 [3, 4096], replicated, may hold values from 2 to 16, as said below
- frequencies: float32 [4096], replicated, may hold values from 2 to 300, as said below
- damping: float32 [4096], replicated, may hold values from 0.015 to 0.03, as said below
- recovery: bfloat16 [2048, 8, 4, 3], P('dom'), may hold values from -1.75 to 1.75
- connectivity: int32 [2048, 4], P('dom'), may hold values from 0 to 383
- node_count: int32 [2048], P('dom'), may hold values from 2 to 4
- shared: int32 [2, 2048], P(None, 'dom'), may hold values from 0 to 255
Outputs:
- response: float32 [16384], P('dom')
The draws below stay inside these ranges and needn't reach their ends.
Inputs may be any that keep to these rules, and one draw needn't show every extreme that they name: Positive node masses. Positive spectral displacements. Positive circular frequencies. Positive damping ratios. `connectivity`: codes below 256 are own nodes; the next 64 codes name the lower neighbour's upper list, the last 64 the upper neighbour's lower list. `shared`: local node numbers; entries may repeat.
All inputs are finite; a program needn't handle non-finite values.
Results may differ from the reference program's by a relative error of at most 0.0025.
Values may be sent and summed in bfloat16 or wider, within the bound.
A program may use at most 64 MiB of HBM per device.

```python
import math
import jax
import jax.numpy as jnp
from jax import lax

M = 4096
CPE = 8
SLOTS = 4
ELEM_DEV = 64
NODE_DEV = 256
SHARE = 64
ELEMS = 2048
NODES = 8192
COMP = 16384
N_DOM = 32


close_count = 8


def close_modes(key):
    ranking = jax.random.permutation(jax.random.fold_in(key, 101), M)
    return ranking < close_count


def draw_masses(key, part):
    position = jnp.arange(NODES, dtype=jnp.float32) / NODES
    rising = jnp.exp(math.log(3.0) * (1.0 - position))
    spread = jnp.exp(jax.random.uniform(key, (NODES,), jnp.float32, math.log(0.5), math.log(2.0)))
    return (rising * spread).astype(jnp.float32)


def draw_frequencies(key, part):
    chosen = close_modes(key)
    low_key = jax.random.fold_in(key, 102)
    high_key = jax.random.fold_in(key, 103)
    close_band = jnp.exp(jax.random.uniform(low_key, (M,), jnp.float32, math.log(2.0), math.log(2.2)))
    broad_band = jnp.exp(jax.random.uniform(high_key, (M,), jnp.float32, math.log(2.4), math.log(300.0)))
    return jnp.where(chosen, close_band, broad_band).astype(jnp.float32)


def draw_spectral(key, part):
    chosen = close_modes(key)
    broad_key = jax.random.fold_in(key, 104)
    strong_key = jax.random.fold_in(key, 105)
    broad_band = jnp.exp(jax.random.uniform(broad_key, (3, M), jnp.float32, math.log(2.0), math.log(4.0)))
    strong = jax.random.uniform(strong_key, (3, M), jnp.float32, 14.0, 16.0)
    return jnp.where(chosen[None, :], strong, broad_band).astype(jnp.float32)


def draw_damping(key, part):
    rate_key = jax.random.fold_in(key, 106)
    rates = jnp.exp(jax.random.uniform(rate_key, (M,), jnp.float32, math.log(0.015), math.log(0.03)))
    return rates.astype(jnp.float32)


def place_ends(result, key, smallest, largest):
    longest = result.shape.index(max(result.shape))
    spots = []
    for shift in (0, 1):
        where = [jax.random.randint(jax.random.fold_in(key, axis), (), 0, length) for axis, length in enumerate(result.shape)]
        where[longest] = (where[longest] + shift) % result.shape[longest]
        spots.append(tuple(where))
    return result.at[spots[0]].set(smallest).at[spots[1]].set(largest)


def levels(rng, dims, cuts, smallest, largest):
    def one(dim, shards_of):
        draws = jax.random.uniform(jax.random.fold_in(jax.random.fold_in(rng, 6), dim), (shards_of,), jnp.float32, smallest / len(cuts), largest / len(cuts))
        return jnp.repeat(jnp.exp(draws), dims[dim] // shards_of).reshape((-1,) + (1,) * (len(dims) - dim - 1))

    level = one(*cuts[0])
    for cut in cuts[1:]:
        level = level * one(*cut)
    return level


def scatter_about(stream_key, dims, scale, limit, cuts=(), held_as=jnp.bfloat16):
    result = scale * jax.random.normal(stream_key, dims, jnp.float32)
    if cuts:
        result = result * levels(stream_key, dims, cuts, -0.22, 0.18)
    return jnp.clip(result, -limit, limit).astype(held_as)


def setup_inputs(seed: int = 0) -> dict:
    seeds = jax.random.split(jax.random.key(seed), 10)
    shapes = scatter_about(seeds[0], (3, NODES, M), 1.0, 6.0, ((1, 32), (2, 16)))
    masses = draw_masses(jax.random.fold_in(seeds[9], 71), 0)
    spectral = draw_spectral(jax.random.fold_in(seeds[9], 71), 0)
    frequencies = draw_frequencies(jax.random.fold_in(seeds[9], 71), 0)
    damping = draw_damping(jax.random.fold_in(seeds[9], 71), 0)
    recovery = scatter_about(seeds[5], (ELEMS, CPE, SLOTS, 3), 12 ** -0.5, 1.75, ((0, 32),))
    connectivity = place_ends(jax.random.randint(seeds[6], (ELEMS, SLOTS), 0, NODE_DEV + 2 * SHARE), jax.random.fold_in(seeds[6], 1), 0, (NODE_DEV + 2 * SHARE) - 1).astype(jnp.int32)
    node_count = place_ends(jax.random.randint(seeds[7], (ELEMS,), 2, SLOTS + 1), jax.random.fold_in(seeds[7], 1), 2, SLOTS).astype(jnp.int32)
    shared = place_ends(jax.random.randint(seeds[8], (2, SHARE * N_DOM), 0, NODE_DEV), jax.random.fold_in(seeds[8], 1), 0, NODE_DEV - 1).astype(jnp.int32)
    return {"shapes": shapes, "masses": masses, "spectral": spectral, "frequencies": frequencies, "damping": damping, "recovery": recovery, "connectivity": connectivity, "node_count": node_count, "shared": shared}


def correlation_weights(amp_rows, amp_cols, freq_rows, freq_cols, rate_rows, rate_cols):
    ratio = freq_cols[None, :] / freq_rows[:, None]
    ratio_sq = ratio * ratio
    rate_row = rate_rows[:, None]
    rate_col = rate_cols[None, :]
    top_part = 8.0 * jnp.sqrt(rate_row * rate_col) * (rate_row + ratio * rate_col) * ratio * jnp.sqrt(ratio)
    spread = 1.0 - ratio_sq
    bottom_part = spread * spread + 4.0 * rate_row * rate_col * ratio * (1.0 + ratio_sq) + 4.0 * (rate_row * rate_row + rate_col * rate_col) * ratio_sq
    correlation = top_part / bottom_part
    return (amp_rows[:, None] * correlation * amp_cols[None, :]).astype(jnp.bfloat16)

def reference(shapes, masses, spectral, frequencies, damping, recovery, connectivity, node_count, shared):
    shape_wide = shapes.astype(jnp.float32)
    weighted = masses[None, :, None] * shape_wide
    lever_arm = lax.optimization_barrier(jnp.sum(weighted, axis=1))
    general = lax.optimization_barrier(jnp.sum(weighted * shape_wide, axis=(0, 1)))
    amplitudes = lever_arm / general[None, :] * spectral
    partition = (jnp.arange(ELEMS) // ELEM_DEV).astype(jnp.int32)[:, None]
    node_code = connectivity.astype(jnp.int32)
    local_node = partition * NODE_DEV + node_code
    low_slot = jnp.clip(node_code - NODE_DEV, 0, SHARE - 1)
    high_slot = jnp.clip(node_code - NODE_DEV - SHARE, 0, SHARE - 1)
    low_part = jnp.clip(partition - 1, 0, N_DOM - 1)
    high_part = jnp.clip(partition + 1, 0, N_DOM - 1)
    low_node = low_part * NODE_DEV + shared[1][low_part * SHARE + low_slot]
    high_node = high_part * NODE_DEV + shared[0][high_part * SHARE + high_slot]
    is_local = node_code < NODE_DEV
    is_low = jnp.logical_and(node_code >= NODE_DEV, node_code < NODE_DEV + SHARE)
    is_high = jnp.logical_and(jnp.logical_not(is_local), jnp.logical_not(is_low))
    node_index = jnp.where(is_local, local_node, jnp.where(is_low, low_node, high_node)).astype(jnp.int32)
    present = is_local | is_low & (partition > 0) | is_high & (partition < N_DOM - 1)
    gathered = jnp.take(shapes, node_index.reshape(-1), axis=1).reshape(3, ELEMS, SLOTS, M)
    gathered = jnp.where(present[None, :, :, None], gathered, jnp.zeros_like(gathered))
    slot_live = (jnp.arange(SLOTS)[None, :] < node_count[:, None]).astype(jnp.bfloat16)
    masked = recovery * slot_live[:, None, :, None]
    forces = jnp.einsum('ekna,aenm->ekm', masked.astype(jnp.float32), gathered.astype(jnp.float32))
    forces = forces.astype(jnp.bfloat16).reshape(COMP, M)
    force_wide = forces.astype(jnp.float32)
    summed = jnp.zeros((COMP,), jnp.float32)
    for direction in range(3):
        weights = correlation_weights(amplitudes[direction], amplitudes[direction], frequencies, frequencies, damping, damping)
        projected = jnp.dot(force_wide, weights.astype(jnp.float32), precision=lax.Precision.HIGHEST, preferred_element_type=jnp.float32)
        summed = summed + lax.optimization_barrier(jnp.sum(projected * force_wide, axis=1))
    return summed
```

```python
import functools

import jax
import jax.numpy as jnp
from jax import lax
from jax.experimental import pallas as pl
from jax.experimental.pallas import tpu as pltpu
from jax.sharding import PartitionSpec as P

MESH = pl.DeviceIdType.MESH
F32 = jnp.float32
BF16 = jnp.bfloat16
CORES = 2


def dot(a, b):
    return jnp.dot(a, b, preferred_element_type=F32)


def offset_of(step):
    return ((step + 1) // 2) * (2 * (step % 2) - 1)


def kernel(
    dims,
    shapes_h, mass_h, spec_h, freq_h, damp_h, rec_h, conn_h, cnt_h, shd_h,
    out_ref,
    shapes, mass, spec, freq, damp, rec, conn, cnt, shd, codes, in_sem,
    half_u, rate_w, rows_u, rows_a, corr,
    halo_out, halo_in, halo_send, halo_recv,
    lev_own, lev_x, lev_z, lx_send, lx_recv, lz_send, lz_recv,
    onehot, recov, gathered, forces, far, f_send, f_recv,
    gain_own, gains, g_send, g_recv,
    scaled, total, res_own, results, r_send, r_recv,
):
    nz, nx, ny = dims
    n_dom, n_mode = nz * nx, ny * CORES
    block = shapes_h.shape[2]
    nodes = shapes_h.shape[1]
    elems = conn_h.shape[1]
    slots = conn_h.shape[0]
    share = shd_h.shape[1]
    comps = forces.shape[0]
    part = comps // n_mode
    wide = CORES * block

    dom = lax.axis_index("dom")
    mode = lax.axis_index("mode")
    zi, xi = dom // nx, dom % nx
    yi, core = mode // CORES, mode % CORES
    up = (dom + 1) % n_dom
    down = (dom + n_dom - 1) % n_dom

    def x_peer(k):
        return zi * nx + (xi + k) % nx

    def z_peer(k):
        return ((zi + k) % nz) * nx + xi

    barrier = pltpu.get_barrier_semaphore()

    def greet(d, m):
        pl.semaphore_signal(barrier, inc=1, device_id=(d, m), device_id_type=MESH)

    greet(up, mode)
    greet(down, mode)
    for k in range(1, nx):
        greet(x_peer(k), mode)
    for k in range(1, nz):
        greet(z_peer(k), mode)
    for k in range(1, n_mode):
        greet(dom, (mode + k) % n_mode)

    own = pl.multiple_of(mode * block, block)
    pairs = [
        (conn_h, conn),
        (cnt_h, cnt),
        (shd_h, shd),
        (shapes_h, shapes),
        (mass_h, mass),
        (spec_h.at[:, pl.ds(own, block)], spec),
        (freq_h, freq),
        (damp_h, damp),
        (rec_h, rec),
    ]
    loads = [pltpu.make_async_copy(a, b, in_sem.at[i]) for i, (a, b) in enumerate(pairs)]
    for load in loads:
        load.start()
    for load in loads:
        load.wait()

    codes[...] = jnp.zeros_like(codes)
    codes[pl.ds(0, slots), pl.ds(0, elems)] = conn[...].astype(F32)
    codes[pl.ds(slots, 1), pl.ds(0, elems)] = cnt[...].astype(F32)
    codes[pl.ds(slots + 1, 2), pl.ds(0, share)] = shd[...].astype(F32)
    columns = jnp.transpose(codes[...])
    node_lane = lax.broadcasted_iota(jnp.int32, (share, nodes), 1).astype(F32)
    pick = jnp.concatenate(
        [
            jnp.where(columns[0:share, slots + 1 + side : slots + 2 + side] == node_lane, 1.0, 0.0)
            for side in range(2)
        ],
        axis=0,
    ).astype(BF16)
    for d in range(3):
        halo_out[d] = dot(pick, shapes[d]).astype(BF16)

    m0 = mass[...]
    hi = m0.astype(BF16).astype(F32)
    mid = (m0 - hi).astype(BF16).astype(F32)
    low = m0 - hi - mid
    row8 = lax.broadcasted_iota(jnp.int32, (8, nodes), 0)
    mass3 = jnp.where(row8 == 0, hi, jnp.where(row8 == 1, mid, jnp.where(row8 == 2, low, 0.0)))
    mass3 = mass3.astype(BF16)
    terms = []
    square = jnp.zeros((8, block), F32)
    for d in range(3):
        terms.append(jnp.sum(dot(mass3, shapes[d]), axis=0, keepdims=True))
        s = shapes[d].astype(F32)
        s2 = s * s
        s2h = s2.astype(BF16)
        s2l = (s2 - s2h.astype(F32)).astype(BF16)
        square = square + dot(mass3, s2h) + dot(mass3, s2l)
    terms.append(jnp.sum(square, axis=0, keepdims=True))
    stack = jnp.concatenate(terms, axis=0)
    half = block // 2
    lev_own[...] = jnp.concatenate([stack[:, :half], stack[:, half:]], axis=0)

    pl.semaphore_wait(barrier, 2 + (nx - 1) + (nz - 1) + (n_mode - 1))

    halo_copies = [
        pltpu.make_async_remote_copy(
            src_ref=halo_out.at[:, pl.ds(share, share)],
            dst_ref=halo_in.at[:, pl.ds(0, share)],
            send_sem=halo_send.at[0],
            recv_sem=halo_recv.at[0],
            device_id=(up, mode),
            device_id_type=MESH,
        ),
        pltpu.make_async_remote_copy(
            src_ref=halo_out.at[:, pl.ds(0, share)],
            dst_ref=halo_in.at[:, pl.ds(share, share)],
            send_sem=halo_send.at[1],
            recv_sem=halo_recv.at[1],
            device_id=(down, mode),
            device_id_type=MESH,
        ),
    ]
    for copy in halo_copies:
        copy.start()
    x_copies = [
        pltpu.make_async_remote_copy(
            src_ref=lev_own,
            dst_ref=lev_x.at[k - 1],
            send_sem=lx_send.at[k - 1],
            recv_sem=lx_recv.at[k - 1],
            device_id=(x_peer(k), mode),
            device_id_type=MESH,
        )
        for k in range(1, nx)
    ]
    for copy in x_copies:
        copy.start()

    table_lane = lax.broadcasted_iota(jnp.int32, (elems, nodes + 2 * share), 1).astype(F32)
    for s in range(slots):
        code = columns[0:elems, s : s + 1]
        live = columns[0:elems, slots : slots + 1] > s
        is_low = jnp.logical_and(code >= nodes, code < nodes + share)
        is_high = code >= nodes + share
        ground_low = jnp.where(is_low, jnp.where(dom == 0, 1.0, 0.0), 0.0)
        ground_high = jnp.where(is_high, jnp.where(dom == n_dom - 1, 1.0, 0.0), 0.0)
        kept = jnp.where(live, 1.0, 0.0) * (1.0 - ground_low) * (1.0 - ground_high)
        code = jnp.where(kept > 0.5, code, -1.0)
        onehot[pl.ds(s * elems, elems)] = jnp.where(code == table_lane, 1.0, 0.0).astype(BF16)

    per = comps // elems
    rec_wide = rec[...].astype(F32)
    lane_elem = lax.broadcasted_iota(jnp.int32, rec_wide.shape, 1) % elems
    for e in range(0, elems, 2):
        recov[pl.ds(e * per, 2 * per)] = jnp.concatenate(
            [jnp.where(lane_elem == e + i, rec_wide, 0.0) for i in range(2)], axis=0
        ).astype(BF16)

    w = freq[...]
    half_u[...] = w * w * 0.25
    rate_w[...] = damp[...] * w
    groups = freq.shape[0]
    u_t = jnp.transpose(half_u[...])
    a_t = jnp.transpose(rate_w[...])
    for g in range(groups):
        rows_u[pl.ds(g * 128, 128)] = jnp.broadcast_to(u_t[:, g : g + 1], (128, 128))
        rows_a[pl.ds(g * 128, 128)] = jnp.broadcast_to(a_t[:, g : g + 1], (128, 128))

    def correlate(row_step, col_step):
        row_chip = (yi + offset_of(row_step) + ny) % ny
        col_chip = (yi + offset_of(col_step) + ny) % ny
        at = col_step * (col_step + 1) // 2 + row_step
        per_chip = wide // 128
        us = [half_u[pl.ds(col_chip * per_chip + g, 1)] for g in range(per_chip)]
        vs = [rate_w[pl.ds(col_chip * per_chip + g, 1)] for g in range(per_chip)]
        chunk = 64

        def rows(r, _):
            first = pl.multiple_of(row_chip * wide + r * chunk, chunk)
            u = rows_u[pl.ds(first, chunk)]
            a = rows_a[pl.ds(first, chunk)]
            for g in range(per_chip):
                gap = u - us[g]
                both = a + vs[g]
                bottom = gap * gap + both * (a * us[g] + vs[g] * u)
                value = both * pltpu.reciprocal(bottom, approx=True)
                corr[at, pl.ds(pl.multiple_of(r * chunk, chunk), chunk), pl.ds(g * 128, 128)] = (
                    value.astype(BF16)
                )
            return 0

        lax.fori_loop(0, wide // chunk, rows, 0)

    def correlate_columns(first, last):
        def column(t, _):
            def row(p, _):
                correlate(p, t)
                return 0

            lax.fori_loop(0, t + 1, row, 0)
            return 0

        lax.fori_loop(first, last, column, 0)

    parts = slots * elems
    for d in range(3):
        gathered[pl.ds(d * parts, parts)] = dot(onehot[:, pl.ds(0, nodes)], shapes[d]).astype(BF16)

    for copy in x_copies:
        copy.wait_recv()
    lev_sum = lev_own[...]
    for k in range(nx - 1):
        lev_sum = lev_sum + lev_x[k]
    lev_z[nz - 1] = lev_sum
    z_copies = [
        pltpu.make_async_remote_copy(
            src_ref=lev_z.at[nz - 1],
            dst_ref=lev_z.at[k - 1],
            send_sem=lz_send.at[k - 1],
            recv_sem=lz_recv.at[k - 1],
            device_id=(z_peer(k), mode),
            device_id_type=MESH,
        )
        for k in range(1, nz)
    ]
    for copy in z_copies:
        copy.start()

    for copy in halo_copies:
        copy.wait_recv()
    for d in range(3):
        far_part = dot(onehot[:, pl.ds(nodes, 2 * share)], halo_in[d]).astype(BF16)
        gathered[pl.ds(d * parts, parts)] = gathered[pl.ds(d * parts, parts)] + far_part
    forces[...] = dot(recov[...], gathered[...]).astype(BF16)

    def mode_of(step, c):
        return ((yi - offset_of(step) + ny) % ny) * CORES + c

    def far_copy(step, c):
        m = mode_of(step, c)
        return pltpu.make_async_remote_copy(
            src_ref=forces.at[pl.ds(pl.multiple_of(m * part, part), part)],
            dst_ref=far.at[step, core],
            send_sem=f_send.at[step, c],
            recv_sem=f_recv.at[step, core],
            device_id=(dom, m),
            device_id_type=MESH,
        )

    def gain_copy(step, c):
        m = mode_of(step, c)
        return pltpu.make_async_remote_copy(
            src_ref=gain_own.at[pl.ds(0, 6)],
            dst_ref=gains.at[step, core, pl.ds(0, 6)],
            send_sem=g_send.at[step, c],
            recv_sem=g_recv.at[step, core],
            device_id=(dom, m),
            device_id_type=MESH,
        )

    def arrival(buffer, sem, step, c):
        return pltpu.make_async_copy(buffer, buffer, sem.at[step, c])

    def start_all(make):
        make(0, 1 - core).start()

        def one(i, _):
            make(i // CORES, i % CORES).start()
            return 0

        lax.fori_loop(CORES, n_mode, one, 0)

    start_all(far_copy)
    far[0, core] = forces[pl.ds(pl.multiple_of(mode * part, part), part)]

    split = max(1, (ny * 5) // 8)
    correlate_columns(0, split)

    for copy in z_copies:
        copy.wait_recv()
    lev_all = lev_z[nz - 1]
    for k in range(nz - 1):
        lev_all = lev_all + lev_z[k]
    w2 = freq[pl.ds(mode * 2, 2)]
    scale2 = jnp.sqrt(0.5 * damp[pl.ds(mode * 2, 2)]) * (w2 * jnp.sqrt(w2))
    sp = spec[...]
    for h in range(2):
        rows = lev_all[4 * h : 4 * h + 3] / lev_all[4 * h + 3 : 4 * h + 4]
        rows = rows * sp[:, h * half : (h + 1) * half] * scale2[h : h + 1]
        gain_own[pl.ds(3 * h, 3)] = rows
    start_all(gain_copy)
    gains[0, core, pl.ds(0, 6)] = gain_own[pl.ds(0, 6)]

    correlate_columns(split, ny)

    total[...] = jnp.zeros_like(total)

    def combine(step):
        pieces = []
        for c in range(CORES):
            f = far[step, c].astype(F32)
            g = gains[step, c]
            for d in range(3):
                for h in range(2):
                    zz = f[:, h * half : (h + 1) * half] * g[3 * h + d : 3 * h + d + 1]
                    scaled[
                        step, pl.ds(d * part, part), pl.ds(c * block + h * half, half)
                    ] = zz.astype(BF16)

        def earlier(p, acc):
            at = step * (step + 1) // 2 + p
            return acc + dot(scaled[p], corr[at])

        acc = lax.fori_loop(0, step, earlier, jnp.zeros((3 * part, wide), F32))
        acc = acc * 2.0 + dot(scaled[step], corr[step * (step + 1) // 2 + step])
        acc = acc * scaled[step].astype(F32)
        add = acc[:, 0:128]
        for g in range(1, wide // 128):
            add = add + acc[:, g * 128 : (g + 1) * 128]
        total[...] += add

    arrival(far.at[0, 1 - core], f_recv, 0, 1 - core).wait()
    arrival(gains.at[0, 1 - core, pl.ds(0, 6)], g_recv, 0, 1 - core).wait()
    combine(0)

    def later(step, _):
        for c in range(CORES):
            arrival(far.at[step, c], f_recv, step, c).wait()
            arrival(gains.at[step, c, pl.ds(0, 6)], g_recv, step, c).wait()
        combine(step)
        return 0

    lax.fori_loop(1, ny, later, 0)

    t32 = total[pl.ds(0, part)]
    for d in range(1, 3):
        t32 = t32 + total[pl.ds(d * part, part)]
    copies = 128 // part
    turned = jnp.transpose(jnp.concatenate([t32] * copies, axis=0))
    line = jnp.sum(turned, axis=0, keepdims=True)
    lane = lax.broadcasted_iota(jnp.int32, (1, 128), 1)
    res_own[...] = jnp.where(lane // part == mode % copies, line, 0.0)
    results[pl.ds(mode, 1)] = res_own[...]

    def result_copy(k):
        return pltpu.make_async_remote_copy(
            src_ref=res_own,
            dst_ref=results.at[pl.ds(mode, 1)],
            send_sem=r_send.at[k],
            recv_sem=r_recv.at[mode],
            device_id=(dom, (mode + k) % n_mode),
            device_id_type=MESH,
        )

    def send_result(k, _):
        result_copy(k).start()
        return 0

    lax.fori_loop(1, n_mode, send_result, 0)

    def get_result(k, _):
        m = (mode + k) % n_mode
        row = results.at[pl.ds(m, 1)]
        pltpu.make_async_copy(row, row, r_recv.at[m]).wait()
        return 0

    lax.fori_loop(1, n_mode, get_result, 0)
    for i in range(n_mode // copies):
        out_ref[pl.ds(i, 1)] = jnp.sum(results[pl.ds(i * copies, copies)], axis=0, keepdims=True)

    for copy in halo_copies + x_copies + z_copies:
        copy.wait_send()

    def sent(i, _):
        far_copy(i // CORES, i % CORES).wait_send()
        gain_copy(i // CORES, i % CORES).wait_send()
        return 0

    far_copy(0, 1 - core).wait_send()
    gain_copy(0, 1 - core).wait_send()
    lax.fori_loop(CORES, n_mode, sent, 0)

    def result_sent(k, _):
        result_copy(k).wait_send()
        return 0

    lax.fori_loop(1, n_mode, result_sent, 0)


def per_device(
    dims, shapes, masses, spectral, frequencies, damping, recovery, connectivity, node_count, shared
):
    nz, nx, ny = dims
    n_mode = ny * CORES
    _, nodes, block = shapes.shape
    elems, slots = connectivity.shape
    per = recovery.shape[1]
    share = shared.shape[1]
    modes = frequencies.shape[0]
    comps = elems * per
    part = comps // n_mode
    wide = CORES * block
    parts = slots * elems
    groups = modes // 128
    dma = pltpu.SemaphoreType.DMA
    vmem = pltpu.VMEM
    scratch = [
        vmem((3, nodes, block), BF16),
        vmem((1, nodes), F32),
        vmem((3, block), F32),
        vmem((groups, 128), F32),
        vmem((groups, 128), F32),
        vmem((per, 3 * parts), BF16),
        vmem((slots, elems), jnp.int32),
        vmem((1, elems), jnp.int32),
        vmem((2, share), jnp.int32),
        vmem((8, 128), F32),
        dma((9,)),
        vmem((groups, 128), F32),
        vmem((groups, 128), F32),
        vmem((modes, 128), F32),
        vmem((modes, 128), F32),
        vmem((ny * (ny + 1) // 2, wide, wide), BF16),
        vmem((3, 2 * share, block), BF16),
        vmem((3, 2 * share, block), BF16),
        dma((2,)),
        dma((2,)),
        vmem((8, block // 2), F32),
        vmem((nx - 1, 8, block // 2), F32),
        vmem((nz, 8, block // 2), F32),
        dma((nx - 1,)),
        dma((nx - 1,)),
        dma((nz - 1,)),
        dma((nz - 1,)),
        vmem((parts, nodes + 2 * share), BF16),
        vmem((comps, 3 * parts), BF16),
        vmem((3 * parts, block), BF16),
        vmem((comps, block), BF16),
        vmem((ny, CORES, part, block), BF16),
        dma((ny, CORES)),
        dma((ny, CORES)),
        vmem((8, block // 2), F32),
        vmem((ny, CORES, 8, block // 2), F32),
        dma((ny, CORES)),
        dma((ny, CORES)),
        vmem((ny, 3 * part, wide), BF16),
        vmem((3 * part, 128), F32),
        vmem((1, 128), F32),
        vmem((n_mode, 128), F32),
        dma((n_mode,)),
        dma((n_mode,)),
    ]
    out = pl.pallas_call(
        functools.partial(kernel, dims),
        out_shape=jax.ShapeDtypeStruct((comps // 128, 128), F32),
        in_specs=[pl.BlockSpec(memory_space=pl.ANY)] * 9,
        out_specs=pl.BlockSpec(memory_space=pltpu.VMEM),
        scratch_shapes=scratch,
        compiler_params=pltpu.CompilerParams(
            collective_id=0, has_side_effects=True, vmem_limit_bytes=48 * 1024 * 1024
        ),
    )(
        shapes,
        masses.reshape(1, nodes),
        spectral,
        frequencies.reshape(groups, 128),
        damping.reshape(groups, 128),
        recovery.transpose(1, 3, 2, 0).reshape(per, 3 * parts),
        connectivity.transpose(1, 0),
        node_count.reshape(1, elems),
        shared,
    )
    return out.reshape(comps)


def solution(mesh, dims=(4, 8, 8)):
    in_specs = (
        P(None, "dom", "mode"),
        P("dom"),
        P(),
        P(),
        P(),
        P("dom", None, None, None),
        P("dom", None),
        P("dom"),
        P(None, "dom"),
    )
    return jax.shard_map(
        functools.partial(per_device, dims),
        mesh=mesh,
        in_specs=in_specs,
        out_specs=P("dom"),
        check_vma=False,
    )
```

```python
import functools

import jax
import jax.numpy as jnp
from jax import lax
from jax.experimental import pallas as pl
from jax.experimental.pallas import tpu as pltpu
from jax.sharding import PartitionSpec as P

MESH = pl.DeviceIdType.MESH
F32 = jnp.float32
BF16 = jnp.bfloat16
CORES = 2
FEATS = 32
CHUNK = 512


def dot(a, b):
    return jnp.dot(a, b, preferred_element_type=F32)


def pieces_of(x, count):
    parts = []
    for _ in range(count):
        parts.append(x.astype(BF16).astype(F32))
        x = x - parts[-1]
    return parts


def offset_of(step):
    return ((step + 1) // 2) * (2 * (step % 2) - 1)


def kernel(
    dims,
    shapes_h, mass_h, spec_h, freq_h, damp_h, rec_h, conn_h, cnt_h, shd_h,
    out_ref,
    shapes, mass, spec, freq, damp, rec, rec_rows, rec_line, conn, cnt, shd, codes, in_sem,
    rate_w, row_feats, col_feats, row_mat, col_mat, rows_a, corr,
    halo_out, halo_in, halo_send, halo_recv,
    lev_own, lev_x, lev_z, lx_send, lx_recv, lz_send, lz_recv,
    onehot, recov, gathered, forces, far, f_send, f_recv,
    gain_own, gains, g_send, g_recv,
    scaled, total, res_own, results, r_send, r_recv,
):
    nz, nx, ny = dims
    n_dom, n_mode = nz * nx, ny * CORES
    block = shapes_h.shape[2]
    nodes = shapes_h.shape[1]
    elems = conn_h.shape[1]
    slots = conn_h.shape[0]
    share = shd_h.shape[1]
    comps = forces.shape[0]
    part = comps // n_mode
    wide = CORES * block

    dom = lax.axis_index("dom")
    mode = lax.axis_index("mode")
    zi, xi = dom // nx, dom % nx
    yi, core = mode // CORES, mode % CORES
    up = (dom + 1) % n_dom
    down = (dom + n_dom - 1) % n_dom

    def x_peer(k):
        return zi * nx + (xi + k) % nx

    def z_peer(k):
        return ((zi + k) % nz) * nx + xi

    barrier = pltpu.get_barrier_semaphore()

    def greet(d, m):
        pl.semaphore_signal(barrier, inc=1, device_id=(d, m), device_id_type=MESH)

    greet(up, mode)
    greet(down, mode)
    for k in range(1, nx):
        greet(x_peer(k), mode)
    for k in range(1, nz):
        greet(z_peer(k), mode)
    for k in range(1, n_mode):
        greet(dom, (mode + k) % n_mode)

    own = pl.multiple_of(mode * block, block)
    pairs = [
        (conn_h, conn),
        (cnt_h, cnt),
        (shd_h, shd),
        (shapes_h, shapes),
        (mass_h, mass),
        (spec_h.at[:, pl.ds(own, block)], spec),
        (freq_h, freq),
        (damp_h, damp),
        (rec_h, rec),
    ]
    loads = [pltpu.make_async_copy(a, b, in_sem.at[i]) for i, (a, b) in enumerate(pairs)]
    for load in loads:
        load.start()
    for load in loads:
        load.wait()

    codes[...] = jnp.zeros_like(codes)
    codes[pl.ds(0, slots), pl.ds(0, elems)] = conn[...].astype(F32)
    codes[pl.ds(slots, 1), pl.ds(0, elems)] = cnt[...].astype(F32)
    codes[pl.ds(slots + 1, 2), pl.ds(0, share)] = shd[...].astype(F32)
    columns = jnp.transpose(codes[...])
    node_lane = lax.broadcasted_iota(jnp.int32, (share, nodes), 1).astype(F32)
    pick = jnp.concatenate(
        [
            jnp.where(columns[0:share, slots + 1 + side : slots + 2 + side] == node_lane, 1.0, 0.0)
            for side in range(2)
        ],
        axis=0,
    ).astype(BF16)
    for d in range(3):
        halo_out[d] = dot(pick, shapes[d]).astype(BF16)

    m0 = mass[...]
    hi = m0.astype(BF16).astype(F32)
    mid = (m0 - hi).astype(BF16).astype(F32)
    low = m0 - hi - mid
    row8 = lax.broadcasted_iota(jnp.int32, (8, nodes), 0)
    mass3 = jnp.where(row8 == 0, hi, jnp.where(row8 == 1, mid, jnp.where(row8 == 2, low, 0.0)))
    mass3 = mass3.astype(BF16)
    terms = []
    square = jnp.zeros((8, block), F32)
    for d in range(3):
        terms.append(jnp.sum(dot(mass3, shapes[d]), axis=0, keepdims=True))
        s = shapes[d].astype(F32)
        s2 = s * s
        s2h = s2.astype(BF16)
        s2l = (s2 - s2h.astype(F32)).astype(BF16)
        square = square + dot(mass3, s2h) + dot(mass3, s2l)
    terms.append(jnp.sum(square, axis=0, keepdims=True))
    stack = jnp.concatenate(terms, axis=0)
    half = block // 2
    lev_own[...] = jnp.concatenate([stack[:, :half], stack[:, half:]], axis=0)

    pl.semaphore_wait(barrier, 2 + (nx - 1) + (nz - 1) + (n_mode - 1))

    halo_copies = [
        pltpu.make_async_remote_copy(
            src_ref=halo_out.at[:, pl.ds(share, share)],
            dst_ref=halo_in.at[:, pl.ds(0, share)],
            send_sem=halo_send.at[0],
            recv_sem=halo_recv.at[0],
            device_id=(up, mode),
            device_id_type=MESH,
        ),
        pltpu.make_async_remote_copy(
            src_ref=halo_out.at[:, pl.ds(0, share)],
            dst_ref=halo_in.at[:, pl.ds(share, share)],
            send_sem=halo_send.at[1],
            recv_sem=halo_recv.at[1],
            device_id=(down, mode),
            device_id_type=MESH,
        ),
    ]
    for copy in halo_copies:
        copy.start()
    x_copies = [
        pltpu.make_async_remote_copy(
            src_ref=lev_own,
            dst_ref=lev_x.at[k - 1],
            send_sem=lx_send.at[k - 1],
            recv_sem=lx_recv.at[k - 1],
            device_id=(x_peer(k), mode),
            device_id_type=MESH,
        )
        for k in range(1, nx)
    ]
    for copy in x_copies:
        copy.start()

    table_lane = lax.broadcasted_iota(jnp.int32, (elems, nodes + 2 * share), 1).astype(F32)
    for s in range(slots):
        code = columns[0:elems, s : s + 1]
        live = columns[0:elems, slots : slots + 1] > s
        is_low = jnp.logical_and(code >= nodes, code < nodes + share)
        is_high = code >= nodes + share
        ground_low = jnp.where(is_low, jnp.where(dom == 0, 1.0, 0.0), 0.0)
        ground_high = jnp.where(is_high, jnp.where(dom == n_dom - 1, 1.0, 0.0), 0.0)
        kept = jnp.where(live, 1.0, 0.0) * (1.0 - ground_low) * (1.0 - ground_high)
        code = jnp.where(kept > 0.5, code, -1.0)
        onehot[pl.ds(s * elems, elems)] = jnp.where(code == table_lane, 1.0, 0.0).astype(BF16)

    per = comps // elems
    for k in range(per):
        for d in range(3):
            rec_rows[pl.ds(d * slots * per + k, slots, stride=per), pl.ds(0, elems)] = rec[k, d].astype(F32)
    for i in range(3 * slots):
        rec_line[:, pl.ds(i * elems, elems)] = rec_rows[pl.ds(i * per, per), pl.ds(0, elems)]
    rec_wide = rec_line[...]
    lane_elem = lax.broadcasted_iota(jnp.int32, rec_wide.shape, 1) % elems
    for e in range(0, elems, 2):
        recov[pl.ds(e * per, 2 * per)] = jnp.concatenate(
            [jnp.where(lane_elem == e + i, rec_wide, 0.0) for i in range(2)], axis=0
        ).astype(BF16)

    groups = freq.shape[0]
    w = freq[...]
    u = w * w * 0.25
    rate = damp[...] * w
    rate_w[...] = rate
    one = jnp.ones_like(w)
    square = pieces_of(u * u, 3)
    u_h, u_m, u_l = pieces_of(u, 3)
    rr_h, rr_m = pieces_of(rate * rate, 2)
    ru_h, ru_m = pieces_of(rate * u, 2)
    r_h, r_m = pieces_of(rate, 2)
    left = [*square, one, one, one, u_h, u_h, u_m, u_m, u_h, u_l]
    right = [one, one, one, *square] + [-2.0 * v for v in (u_h, u_m, u_h, u_m, u_l, u_h)]
    for (p_h, p_m), (q_h, q_m) in (
        ((rr_h, rr_m), (u_h, u_m)),
        ((ru_h, ru_m), (r_h, r_m)),
        ((r_h, r_m), (ru_h, ru_m)),
        ((u_h, u_m), (rr_h, rr_m)),
    ):
        left += [p_h, p_h, p_m]
        right += [q_h, q_m, q_h]
    for feats, values in ((row_feats, left), (col_feats, right)):
        for i in range(FEATS):
            feats[pl.ds(i * groups, groups)] = values[i] if i < len(values) else jnp.zeros_like(w)
    a_t = jnp.transpose(rate)
    for g in range(groups):
        at = pl.ds(g * 128, 128)
        row_mat[at] = jnp.transpose(row_feats[pl.ds(g, FEATS, stride=groups)]).astype(BF16)
        col_mat[:, at] = col_feats[pl.ds(g, FEATS, stride=groups)].astype(BF16)
        rows_a[at] = jnp.broadcast_to(a_t[:, g : g + 1], (128, 128))

    def correlate(row_step, col_step):
        row_chip = (yi + offset_of(row_step) + ny) % ny
        col_chip = (yi + offset_of(col_step) + ny) % ny
        at = col_step * (col_step + 1) // 2 + row_step
        per_chip = wide // 128
        vs = [rate_w[pl.ds(col_chip * per_chip + g, 1)] for g in range(per_chip)]
        cols = col_mat[:, pl.ds(pl.multiple_of(col_chip * wide, wide), wide)]

        def rows(r, _):
            first = pl.multiple_of(row_chip * wide + r * CHUNK, CHUNK)
            bottom = dot(row_mat[pl.ds(first, CHUNK)], cols)
            a = rows_a[pl.ds(first, CHUNK)]
            to = pl.ds(pl.multiple_of(at * wide + r * CHUNK, CHUNK), CHUNK)
            for g in range(per_chip):
                value = (a + vs[g]) * pltpu.reciprocal(bottom[:, g * 128 : (g + 1) * 128], approx=True)
                corr[to, pl.ds(g * 128, 128)] = value.astype(BF16)
            return 0

        lax.fori_loop(0, wide // CHUNK, rows, 0)

    def correlate_columns(first, last):
        def column(t, _):
            def row(p, _):
                correlate(p, t)
                return 0

            lax.fori_loop(0, t + 1, row, 0)
            return 0

        lax.fori_loop(first, last, column, 0)

    parts = slots * elems
    for d in range(3):
        gathered[pl.ds(d * parts, parts)] = dot(onehot[:, pl.ds(0, nodes)], shapes[d]).astype(BF16)

    for copy in x_copies:
        copy.wait_recv()
    lev_sum = lev_own[...]
    for k in range(nx - 1):
        lev_sum = lev_sum + lev_x[k]
    lev_z[nz - 1] = lev_sum
    z_copies = [
        pltpu.make_async_remote_copy(
            src_ref=lev_z.at[nz - 1],
            dst_ref=lev_z.at[k - 1],
            send_sem=lz_send.at[k - 1],
            recv_sem=lz_recv.at[k - 1],
            device_id=(z_peer(k), mode),
            device_id_type=MESH,
        )
        for k in range(1, nz)
    ]
    for copy in z_copies:
        copy.start()

    for copy in halo_copies:
        copy.wait_recv()
    for d in range(3):
        far_part = dot(onehot[:, pl.ds(nodes, 2 * share)], halo_in[d]).astype(BF16)
        gathered[pl.ds(d * parts, parts)] = gathered[pl.ds(d * parts, parts)] + far_part
    forces[...] = dot(recov[...], gathered[...]).astype(BF16)

    def mode_of(step, c):
        return ((yi - offset_of(step) + ny) % ny) * CORES + c

    def far_copy(step, c):
        m = mode_of(step, c)
        return pltpu.make_async_remote_copy(
            src_ref=forces.at[pl.ds(pl.multiple_of(m * part, part), part)],
            dst_ref=far.at[step, core],
            send_sem=f_send.at[step, c],
            recv_sem=f_recv.at[step, core],
            device_id=(dom, m),
            device_id_type=MESH,
        )

    def gain_copy(step, c):
        m = mode_of(step, c)
        return pltpu.make_async_remote_copy(
            src_ref=gain_own.at[pl.ds(0, 6)],
            dst_ref=gains.at[step, core, pl.ds(0, 6)],
            send_sem=g_send.at[step, c],
            recv_sem=g_recv.at[step, core],
            device_id=(dom, m),
            device_id_type=MESH,
        )

    def arrival(buffer, sem, step, c):
        return pltpu.make_async_copy(buffer, buffer, sem.at[step, c])

    def start_all(make):
        make(0, 1 - core).start()

        def one(i, _):
            make(i // CORES, i % CORES).start()
            return 0

        lax.fori_loop(CORES, n_mode, one, 0)

    start_all(far_copy)
    far[0, core] = forces[pl.ds(pl.multiple_of(mode * part, part), part)]

    split = max(1, (ny * 5) // 8)
    correlate_columns(0, split)

    for copy in z_copies:
        copy.wait_recv()
    lev_all = lev_z[nz - 1]
    for k in range(nz - 1):
        lev_all = lev_all + lev_z[k]
    w2 = freq[pl.ds(mode * 2, 2)]
    scale2 = jnp.sqrt(0.5 * damp[pl.ds(mode * 2, 2)]) * (w2 * jnp.sqrt(w2))
    sp = spec[...]
    for h in range(2):
        rows = lev_all[4 * h : 4 * h + 3] / lev_all[4 * h + 3 : 4 * h + 4]
        rows = rows * sp[:, h * half : (h + 1) * half] * scale2[h : h + 1]
        gain_own[pl.ds(3 * h, 3)] = rows
    start_all(gain_copy)
    gains[0, core, pl.ds(0, 6)] = gain_own[pl.ds(0, 6)]

    correlate_columns(split, ny)

    total[...] = jnp.zeros_like(total)

    def combine(step):
        pieces = []
        for c in range(CORES):
            f = far[step, c].astype(F32)
            g = gains[step, c]
            for d in range(3):
                for h in range(2):
                    zz = f[:, h * half : (h + 1) * half] * g[3 * h + d : 3 * h + d + 1]
                    scaled[
                        pl.ds(d * part, part), pl.ds(step * wide + c * block + h * half, half)
                    ] = zz.astype(BF16)
        at = step * (step + 1) // 2 * wide
        here = pl.ds(step * wide, wide)
        acc = dot(scaled[:, here], corr[pl.ds(at + step * wide, wide)])
        if step:
            acc = acc + 2.0 * dot(scaled[:, pl.ds(0, step * wide)], corr[pl.ds(at, step * wide)])
        acc = acc * scaled[:, here].astype(F32)
        add = acc[:, 0:128]
        for g in range(1, wide // 128):
            add = add + acc[:, g * 128 : (g + 1) * 128]
        total[...] += add

    arrival(far.at[0, 1 - core], f_recv, 0, 1 - core).wait()
    arrival(gains.at[0, 1 - core, pl.ds(0, 6)], g_recv, 0, 1 - core).wait()
    combine(0)

    for step in range(1, ny):
        for c in range(CORES):
            arrival(far.at[step, c], f_recv, step, c).wait()
            arrival(gains.at[step, c, pl.ds(0, 6)], g_recv, step, c).wait()
        combine(step)

    t32 = total[pl.ds(0, part)]
    for d in range(1, 3):
        t32 = t32 + total[pl.ds(d * part, part)]
    copies = 128 // part
    turned = jnp.transpose(jnp.concatenate([t32] * copies, axis=0))
    line = jnp.sum(turned, axis=0, keepdims=True)
    lane = lax.broadcasted_iota(jnp.int32, (1, 128), 1)
    res_own[...] = jnp.where(lane // part == mode % copies, line, 0.0)
    results[pl.ds(mode, 1)] = res_own[...]

    def result_copy(k):
        return pltpu.make_async_remote_copy(
            src_ref=res_own,
            dst_ref=results.at[pl.ds(mode, 1)],
            send_sem=r_send.at[k],
            recv_sem=r_recv.at[mode],
            device_id=(dom, (mode + k) % n_mode),
            device_id_type=MESH,
        )

    def send_result(k, _):
        result_copy(k).start()
        return 0

    lax.fori_loop(1, n_mode, send_result, 0)

    def get_result(k, _):
        m = (mode + k) % n_mode
        row = results.at[pl.ds(m, 1)]
        pltpu.make_async_copy(row, row, r_recv.at[m]).wait()
        return 0

    lax.fori_loop(1, n_mode, get_result, 0)
    for i in range(n_mode // copies):
        out_ref[pl.ds(i, 1)] = jnp.sum(results[pl.ds(i * copies, copies)], axis=0, keepdims=True)

    for copy in halo_copies + x_copies + z_copies:
        copy.wait_send()

    def sent(i, _):
        far_copy(i // CORES, i % CORES).wait_send()
        gain_copy(i // CORES, i % CORES).wait_send()
        return 0

    far_copy(0, 1 - core).wait_send()
    gain_copy(0, 1 - core).wait_send()
    lax.fori_loop(CORES, n_mode, sent, 0)

    def result_sent(k, _):
        result_copy(k).wait_send()
        return 0

    lax.fori_loop(1, n_mode, result_sent, 0)


def per_device(
    dims, shapes, masses, spectral, frequencies, damping, recovery, connectivity, node_count, shared
):
    nz, nx, ny = dims
    n_mode = ny * CORES
    _, nodes, block = shapes.shape
    elems, slots = connectivity.shape
    per = recovery.shape[1]
    share = shared.shape[1]
    modes = frequencies.shape[0]
    comps = elems * per
    part = comps // n_mode
    wide = CORES * block
    parts = slots * elems
    groups = modes // 128
    dma = pltpu.SemaphoreType.DMA
    vmem = pltpu.VMEM
    scratch = [
        vmem((3, nodes, block), BF16),
        vmem((1, nodes), F32),
        vmem((3, block), F32),
        vmem((groups, 128), F32),
        vmem((groups, 128), F32),
        vmem((per, 3, slots, elems), BF16),
        vmem((3 * slots * per, 128), F32),
        vmem((per, 3 * parts), F32),
        vmem((slots, elems), jnp.int32),
        vmem((1, elems), jnp.int32),
        vmem((2, share), jnp.int32),
        vmem((8, 128), F32),
        dma((9,)),
        vmem((groups, 128), F32),
        vmem((FEATS * groups, 128), F32),
        vmem((FEATS * groups, 128), F32),
        vmem((modes, FEATS), BF16),
        vmem((FEATS, modes), BF16),
        vmem((modes, 128), F32),
        vmem((ny * (ny + 1) // 2 * wide, wide), BF16),
        vmem((3, 2 * share, block), BF16),
        vmem((3, 2 * share, block), BF16),
        dma((2,)),
        dma((2,)),
        vmem((8, block // 2), F32),
        vmem((nx - 1, 8, block // 2), F32),
        vmem((nz, 8, block // 2), F32),
        dma((nx - 1,)),
        dma((nx - 1,)),
        dma((nz - 1,)),
        dma((nz - 1,)),
        vmem((parts, nodes + 2 * share), BF16),
        vmem((comps, 3 * parts), BF16),
        vmem((3 * parts, block), BF16),
        vmem((comps, block), BF16),
        vmem((ny, CORES, part, block), BF16),
        dma((ny, CORES)),
        dma((ny, CORES)),
        vmem((8, block // 2), F32),
        vmem((ny, CORES, 8, block // 2), F32),
        dma((ny, CORES)),
        dma((ny, CORES)),
        vmem((3 * part, modes), BF16),
        vmem((3 * part, 128), F32),
        vmem((1, 128), F32),
        vmem((n_mode, 128), F32),
        dma((n_mode,)),
        dma((n_mode,)),
    ]
    out = pl.pallas_call(
        functools.partial(kernel, dims),
        out_shape=jax.ShapeDtypeStruct((comps // 128, 128), F32),
        in_specs=[pl.BlockSpec(memory_space=pltpu.HBM)] * 9,
        out_specs=pl.BlockSpec(memory_space=pltpu.VMEM),
        scratch_shapes=scratch,
        compiler_params=pltpu.CompilerParams(
            collective_id=0, has_side_effects=True, vmem_limit_bytes=48 * 1024 * 1024
        ),
    )(
        shapes,
        masses.reshape(1, nodes),
        spectral,
        frequencies.reshape(groups, 128),
        damping.reshape(groups, 128),
        recovery.transpose(1, 3, 2, 0),
        connectivity.transpose(1, 0),
        node_count.reshape(1, elems),
        shared,
    )
    return out.reshape(comps)


def solution(mesh, dims=(4, 8, 8)):
    in_specs = (
        P(None, "dom", "mode"),
        P("dom"),
        P(),
        P(),
        P(),
        P("dom", None, None, None),
        P("dom", None),
        P("dom"),
        P(None, "dom"),
    )
    return jax.shard_map(
        functools.partial(per_device, dims),
        mesh=mesh,
        in_specs=in_specs,
        out_specs=P("dom"),
        check_vma=False,
    )
```

```python
import functools

import jax
import jax.numpy as jnp
from jax import lax
from jax.experimental import pallas as pl
from jax.experimental.pallas import tpu as pltpu
from jax.sharding import PartitionSpec as P

MESH = pl.DeviceIdType.MESH
F32 = jnp.float32
BF16 = jnp.bfloat16
CORES = 2
FEATS = 32
RATE = 24
CHUNK = 256


def dot(a, b):
    return jnp.dot(a, b, preferred_element_type=F32)


def pieces_of(x, count):
    parts = []
    for _ in range(count):
        parts.append(x.astype(BF16).astype(F32))
        x = x - parts[-1]
    return parts


def offset_of(step):
    return ((step + 1) // 2) * (2 * (step % 2) - 1)


def remote(src, dst, send, recv, device):
    return pltpu.make_async_remote_copy(
        src_ref=src,
        dst_ref=dst,
        send_sem=send,
        recv_sem=recv,
        device_id=device,
        device_id_type=MESH,
    )


def kernel(
    dims,
    shapes_h, mass_h, spec_h, freq_h, damp_h, rec_h, conn_h, cnt_h, shd_h,
    out_ref,
    shapes, mass, spec, freq, damp, rec, rec_rows, rec_line, conn, cnt, shd, codes, in_sem,
    rate_w, row_feats, col_feats, row_mat, col_mat, rows_a, corr,
    halo_out, halo_in, halo_send, halo_recv,
    lev_own, lev_x, lev_z, lx_send, lx_recv, lz_send, lz_recv,
    onehot, recov, gathered, near, reach, forces,
    far, f_send, f_pass, f_recv,
    gain_own, gains, g_send, g_pass, g_recv,
    scaled, total, res_own, results, r_send, r_recv,
):
    nz, nx, ny = dims
    n_dom, n_mode = nz * nx, ny * CORES
    block = shapes_h.shape[2]
    half = block // 2
    nodes = shapes_h.shape[1]
    elems = conn_h.shape[1]
    slots = conn_h.shape[0]
    share = shd_h.shape[1]
    comps = forces.shape[0]
    part = comps // ny
    wide = CORES * block

    dom = lax.axis_index("dom")
    mode = lax.axis_index("mode")
    zi, xi = dom // nx, dom % nx
    yi, core = mode // CORES, mode % CORES
    other = 1 - core
    sibling = (dom, yi * CORES + other)
    up = (dom + 1) % n_dom
    down = (dom + n_dom - 1) % n_dom
    chips_from = [(yi + offset_of(s) + ny) % ny for s in range(ny)]
    chips_to = [(yi - offset_of(s) + ny) % ny for s in range(ny)]
    x_peers = [(zi * nx + (xi + k) % nx, mode) for k in range(1, nx)]
    z_peers = [(((zi + k) % nz) * nx + xi, mode) for k in range(1, nz)]
    mode_peers = [(dom, (mode + k) % n_mode) for k in range(1, n_mode)]

    own = pl.multiple_of(mode * block, block)
    pairs = [
        (conn_h, conn),
        (cnt_h, cnt),
        (shd_h, shd),
        (shapes_h, shapes),
        (mass_h, mass),
        (rec_h, rec),
        (freq_h, freq),
        (damp_h, damp),
        (spec_h.at[:, pl.ds(own, block)], spec),
    ]
    loads = [pltpu.make_async_copy(a, b, in_sem.at[i]) for i, (a, b) in enumerate(pairs)]
    for load in loads:
        load.start()

    barrier = pltpu.get_barrier_semaphore()
    greeted = [(up, mode), (down, mode)] + x_peers + z_peers + mode_peers
    for peer in greeted:
        pl.semaphore_signal(barrier, inc=1, device_id=peer, device_id_type=MESH)

    for load in loads[:4]:
        load.wait()

    codes[...] = jnp.zeros_like(codes)
    codes[pl.ds(0, slots), pl.ds(0, elems)] = conn[...].astype(F32)
    codes[pl.ds(slots, 1), pl.ds(0, elems)] = cnt[...].astype(F32)
    codes[pl.ds(slots + 1, 2), pl.ds(0, share)] = shd[...].astype(F32)
    columns = jnp.transpose(codes[...])
    node_lane = lax.broadcasted_iota(jnp.int32, (share, nodes), 1).astype(F32)
    pick = jnp.concatenate(
        [
            jnp.where(columns[0:share, slots + 1 + side : slots + 2 + side] == node_lane, 1.0, 0.0)
            for side in range(2)
        ],
        axis=0,
    ).astype(BF16)
    for d in range(3):
        halo_out[d] = dot(pick, shapes[d]).astype(BF16)

    pl.semaphore_wait(barrier, len(greeted))

    lower, upper = pl.ds(0, share), pl.ds(share, share)
    halo_copies = [
        remote(halo_out.at[:, upper], halo_in.at[:, lower], halo_send.at[0], halo_recv.at[0], (up, mode)),
        remote(halo_out.at[:, lower], halo_in.at[:, upper], halo_send.at[1], halo_recv.at[1], (down, mode)),
    ]
    for copy in halo_copies:
        copy.start()

    for load in loads[4:]:
        load.wait()
    parts3 = pieces_of(mass[...], 3)
    row8 = lax.broadcasted_iota(jnp.int32, (8, nodes), 0)
    mass3 = jnp.zeros((8, nodes), F32)
    for i in range(3):
        mass3 = jnp.where(row8 == i, parts3[i], mass3)
    mass3 = mass3.astype(BF16)
    terms = []
    square = jnp.zeros((8, block), F32)
    for d in range(3):
        terms.append(jnp.sum(dot(mass3, shapes[d]), axis=0, keepdims=True))
        s = shapes[d].astype(F32)
        s2h, s2l = pieces_of(s * s, 2)
        square = square + dot(mass3, s2h.astype(BF16)) + dot(mass3, s2l.astype(BF16))
    terms.append(jnp.sum(square, axis=0, keepdims=True))
    stack = jnp.concatenate(terms, axis=0)
    lev_own[...] = jnp.concatenate([stack[:, :half], stack[:, half:]], axis=0)

    x_copies = [
        remote(lev_own, lev_x.at[k], lx_send.at[k], lx_recv.at[k], peer)
        for k, peer in enumerate(x_peers)
    ]
    for copy in x_copies:
        copy.start()

    table_lane = lax.broadcasted_iota(jnp.int32, (elems, nodes + 2 * share), 1).astype(F32)
    for s in range(slots):
        code = columns[0:elems, s : s + 1]
        live = columns[0:elems, slots : slots + 1] > s
        is_low = jnp.logical_and(code >= nodes, code < nodes + share)
        is_high = code >= nodes + share
        ground_low = jnp.where(is_low, jnp.where(dom == 0, 1.0, 0.0), 0.0)
        ground_high = jnp.where(is_high, jnp.where(dom == n_dom - 1, 1.0, 0.0), 0.0)
        kept = jnp.where(live, 1.0, 0.0) * (1.0 - ground_low) * (1.0 - ground_high)
        code = jnp.where(kept > 0.5, code, -1.0)
        onehot[pl.ds(s * elems, elems)] = jnp.where(code == table_lane, 1.0, 0.0).astype(BF16)

    per = comps // elems
    for k in range(per):
        for d in range(3):
            rec_rows[pl.ds(d * slots * per + k, slots, stride=per), pl.ds(0, elems)] = rec[k, d].astype(F32)
    for i in range(3 * slots):
        rec_line[:, pl.ds(i * elems, elems)] = rec_rows[pl.ds(i * per, per), pl.ds(0, elems)]
    rec_wide = rec_line[...]
    lane_elem = lax.broadcasted_iota(jnp.int32, rec_wide.shape, 1) % elems
    for e in range(0, elems, 2):
        recov[pl.ds(e * per, 2 * per)] = jnp.concatenate(
            [jnp.where(lane_elem == e + i, rec_wide, 0.0) for i in range(2)], axis=0
        ).astype(BF16)

    parts = slots * elems
    for d in range(3):
        gathered[pl.ds(d * parts, parts)] = dot(onehot[:, pl.ds(0, nodes)], shapes[d]).astype(BF16)
        reach[:, pl.ds(d * 2 * share, 2 * share)] = dot(
            recov[:, pl.ds(d * parts, parts)], onehot[:, pl.ds(nodes, 2 * share)]
        ).astype(BF16)
    near[...] = dot(recov[...], gathered[...])

    groups = freq.shape[0]
    w = freq[...]
    u = w * w * 0.25
    rate = damp[...] * w
    rate_w[...] = rate
    one = jnp.ones_like(w)
    uu = pieces_of(u * u, 3)
    u_h, u_m, u_l = pieces_of(u, 3)
    rr = pieces_of(rate * rate, 2)
    ru = pieces_of(rate * u, 2)
    r1 = pieces_of(rate, 2)
    left = [*uu, one, one, one, u_h, u_h, u_m, u_m, u_h, u_l]
    right = [one, one, one, *uu] + [-2.0 * v for v in (u_h, u_m, u_h, u_m, u_l, u_h)]
    for (p_h, p_m), (q_h, q_m) in ((rr, (u_h, u_m)), (ru, r1), (r1, ru), ((u_h, u_m), rr)):
        left += [p_h, p_h, p_m]
        right += [q_h, q_m, q_h]
    zero = jnp.zeros_like(w)
    left += [rate] + [zero] * (FEATS - len(left) - 1)
    right += [zero] * (FEATS - len(right))
    for feats, values in ((row_feats, left), (col_feats, right)):
        for i in range(FEATS):
            feats[pl.ds(i * groups, groups)] = values[i]
    per_chip = wide // 128
    per_core = block // 128
    for step in range(ny):
        for j in range(per_chip):
            g = chips_from[step] * per_chip + j
            at = pl.ds(step * wide + j * 128, 128)
            turned = jnp.transpose(row_feats[pl.ds(g, FEATS, stride=groups)])
            row_mat[at] = turned.astype(BF16)
            rows_a[at] = jnp.broadcast_to(turned[:, RATE : RATE + 1], (128, 128))
        for j in range(per_core):
            g = chips_from[step] * per_chip + core * per_core + j
            col_mat[:, pl.ds(step * block + j * 128, 128)] = col_feats[
                pl.ds(g, FEATS, stride=groups)
            ].astype(BF16)

    def correlate(step):
        base = step * (step + 1) // 2 * wide
        vs = [
            rate_w[pl.ds(chips_from[step] * per_chip + core * per_core + j, 1)]
            for j in range(per_core)
        ]
        cols = col_mat[:, pl.ds(step * block, block)]
        for r in range(0, (step + 1) * wide, CHUNK):
            bottom = dot(row_mat[pl.ds(r, CHUNK)], cols)
            a = rows_a[pl.ds(r, CHUNK)]
            for j in range(per_core):
                value = (a + vs[j]) * pltpu.reciprocal(bottom[:, j * 128 : (j + 1) * 128], approx=True)
                corr[pl.ds(base + r, CHUNK), pl.ds(j * 128, 128)] = value.astype(BF16)

    for step in range(0, 3):
        correlate(step)

    for copy in halo_copies:
        copy.wait_recv()
    forces[...] = (near[...] + dot(reach[...], halo_in[...].reshape(6 * share, block))).astype(BF16)

    def rows_of(chip):
        return forces.at[pl.ds(pl.multiple_of(chip * part, part), part)]

    f_copies = [None] + [
        remote(
            rows_of(chips_to[s]),
            far.at[s, core],
            f_send.at[s],
            f_recv.at[s, core],
            (dom, chips_to[s] * CORES + core),
        )
        for s in range(1, ny)
    ]
    for copy in f_copies[1:]:
        copy.start()
    f_passes = [remote(rows_of(yi), far.at[0, core], f_pass.at[0], f_recv.at[0, core], sibling)] + [
        remote(far.at[s, core], far.at[s, core], f_pass.at[s], f_recv.at[s, core], sibling)
        for s in range(1, ny)
    ]
    f_passes[0].start()
    far[0, core] = forces[pl.ds(pl.multiple_of(yi * part, part), part)]

    for copy in x_copies:
        copy.wait_recv()
    lev_sum = lev_own[...]
    for k in range(nx - 1):
        lev_sum = lev_sum + lev_x[k]
    lev_z[nz - 1] = lev_sum
    z_copies = [
        remote(lev_z.at[nz - 1], lev_z.at[k], lz_send.at[k], lz_recv.at[k], peer)
        for k, peer in enumerate(z_peers)
    ]
    for copy in z_copies:
        copy.start()

    for step in range(3, min(5, ny)):
        correlate(step)

    for copy in z_copies:
        copy.wait_recv()
    lev_all = lev_z[nz - 1]
    for k in range(nz - 1):
        lev_all = lev_all + lev_z[k]
    w2 = freq[pl.ds(mode * per_core, per_core)]
    scale2 = jnp.sqrt(0.5 * damp[pl.ds(mode * per_core, per_core)]) * (w2 * jnp.sqrt(w2))
    sp = spec[...]
    for h in range(2):
        rows = lev_all[4 * h : 4 * h + 3] / lev_all[4 * h + 3 : 4 * h + 4]
        rows = rows * sp[:, h * half : (h + 1) * half] * scale2[h : h + 1]
        gain_own[pl.ds(3 * h, 3)] = rows
    six = pl.ds(0, 6)

    def gain_slot(s):
        return gains.at[s, core, six]

    g_copies = [None] + [
        remote(
            gain_own.at[six],
            gain_slot(s),
            g_send.at[s],
            g_recv.at[s, core],
            (dom, chips_to[s] * CORES + core),
        )
        for s in range(1, ny)
    ]
    for copy in g_copies[1:]:
        copy.start()
    g_passes = [remote(gain_own.at[six], gain_slot(0), g_pass.at[0], g_recv.at[0, core], sibling)] + [
        remote(gain_slot(s), gain_slot(s), g_pass.at[s], g_recv.at[s, core], sibling)
        for s in range(1, ny)
    ]
    g_passes[0].start()
    gains[0, core, six] = gain_own[six]

    def hand_on(s):
        f_copies[s].wait_recv()
        f_passes[s].start()

    def hand_on_gain(s):
        g_copies[s].wait_recv()
        g_passes[s].start()

    done = 1
    for step in range(5, ny):
        correlate(step)
        while done < ny and done <= 2 * (step - 4):
            hand_on(done)
            done += 1
    for s in range(1, ny):
        hand_on_gain(s)
    for s in range(done, ny):
        hand_on(s)

    total[...] = jnp.zeros_like(total)

    def arrival(buffer, sem):
        pltpu.make_async_copy(buffer, buffer, sem).wait()

    for step in range(ny):
        arrival(far.at[step, other], f_recv.at[step, other])
        arrival(gains.at[step, other, six], g_recv.at[step, other])
        for c in range(CORES):
            f = far[step, c].astype(F32)
            g = gains[step, c]
            for d in range(3):
                for h in range(2):
                    zz = f[:, h * half : (h + 1) * half] * g[3 * h + d : 3 * h + d + 1]
                    scaled[
                        pl.ds(d * part, part), pl.ds(step * wide + c * block + h * half, half)
                    ] = zz.astype(BF16)
        base = step * (step + 1) // 2 * wide
        acc = dot(scaled[:, pl.ds(step * wide, wide)], corr[pl.ds(base + step * wide, wide)])
        if step:
            acc = acc + 2.0 * dot(scaled[:, pl.ds(0, step * wide)], corr[pl.ds(base, step * wide)])
        mine = pl.ds(pl.multiple_of(step * wide + core * block, block), block)
        acc = acc * scaled[:, mine].astype(F32)
        add = acc[:, 0:128]
        for j in range(1, per_core):
            add = add + acc[:, j * 128 : (j + 1) * 128]
        total[...] += add

    summed = total[pl.ds(0, part)]
    for d in range(1, 3):
        summed = summed + total[pl.ds(d * part, part)]
    copies = 128 // part
    turned = jnp.transpose(jnp.concatenate([summed] * copies, axis=0))
    line = jnp.sum(turned, axis=0, keepdims=True)
    lane = lax.broadcasted_iota(jnp.int32, (1, 128), 1)
    res_own[...] = jnp.where(lane // part == yi % copies, line, 0.0)

    r_copies = [
        remote(res_own, results.at[pl.ds(mode, 1)], r_send.at[k], r_recv.at[mode], peer)
        for k, peer in enumerate(mode_peers)
    ]
    for copy in r_copies:
        copy.start()
    results[pl.ds(mode, 1)] = res_own[...]
    for _, m in mode_peers:
        arrival(results.at[pl.ds(m, 1)], r_recv.at[m])
    rows_each = n_mode * 128 // comps
    for i in range(comps // 128):
        out_ref[pl.ds(i, 1)] = jnp.sum(results[pl.ds(i * rows_each, rows_each)], axis=0, keepdims=True)

    for copy in halo_copies + x_copies + z_copies + f_copies[1:] + f_passes + g_copies[1:] + g_passes + r_copies:
        copy.wait_send()


def per_device(
    dims, shapes, masses, spectral, frequencies, damping, recovery, connectivity, node_count, shared
):
    nz, nx, ny = dims
    n_mode = ny * CORES
    _, nodes, block = shapes.shape
    elems, slots = connectivity.shape
    per = recovery.shape[1]
    share = shared.shape[1]
    modes = frequencies.shape[0]
    comps = elems * per
    part = comps // ny
    wide = CORES * block
    parts = slots * elems
    groups = modes // 128
    dma = pltpu.SemaphoreType.DMA
    vmem = pltpu.VMEM
    scratch = [
        vmem((3, nodes, block), BF16),
        vmem((1, nodes), F32),
        vmem((3, block), F32),
        vmem((groups, 128), F32),
        vmem((groups, 128), F32),
        vmem((per, 3, slots, elems), BF16),
        vmem((3 * slots * per, 128), F32),
        vmem((per, 3 * parts), F32),
        vmem((slots, elems), jnp.int32),
        vmem((1, elems), jnp.int32),
        vmem((2, share), jnp.int32),
        vmem((8, 128), F32),
        dma((9,)),
        vmem((groups, 128), F32),
        vmem((FEATS * groups, 128), F32),
        vmem((FEATS * groups, 128), F32),
        vmem((modes, FEATS), BF16),
        vmem((FEATS, modes // CORES), BF16),
        vmem((modes, 128), F32),
        vmem((ny * (ny + 1) // 2 * wide, block), BF16),
        vmem((3, 2 * share, block), BF16),
        vmem((3, 2 * share, block), BF16),
        dma((2,)),
        dma((2,)),
        vmem((8, block // 2), F32),
        vmem((nx - 1, 8, block // 2), F32),
        vmem((nz, 8, block // 2), F32),
        dma((nx - 1,)),
        dma((nx - 1,)),
        dma((nz - 1,)),
        dma((nz - 1,)),
        vmem((parts, nodes + 2 * share), BF16),
        vmem((comps, 3 * parts), BF16),
        vmem((3 * parts, block), BF16),
        vmem((comps, block), F32),
        vmem((comps, 6 * share), BF16),
        vmem((comps, block), BF16),
        vmem((ny, CORES, part, block), BF16),
        dma((ny,)),
        dma((ny,)),
        dma((ny, CORES)),
        vmem((8, block // 2), F32),
        vmem((ny, CORES, 8, block // 2), F32),
        dma((ny,)),
        dma((ny,)),
        dma((ny, CORES)),
        vmem((3 * part, modes), BF16),
        vmem((3 * part, 128), F32),
        vmem((1, 128), F32),
        vmem((n_mode, 128), F32),
        dma((n_mode - 1,)),
        dma((n_mode,)),
    ]
    out = pl.pallas_call(
        functools.partial(kernel, dims),
        out_shape=jax.ShapeDtypeStruct((comps // 128, 128), F32),
        in_specs=[pl.BlockSpec(memory_space=pltpu.HBM)] * 9,
        out_specs=pl.BlockSpec(memory_space=pltpu.VMEM),
        scratch_shapes=scratch,
        compiler_params=pltpu.CompilerParams(
            collective_id=0, has_side_effects=True, vmem_limit_bytes=56 * 1024 * 1024
        ),
    )(
        shapes,
        masses.reshape(1, nodes),
        spectral,
        frequencies.reshape(groups, 128),
        damping.reshape(groups, 128),
        recovery.transpose(1, 3, 2, 0),
        connectivity.transpose(1, 0),
        node_count.reshape(1, elems),
        shared,
    )
    return out.reshape(comps)


def solution(mesh, dims=(4, 8, 8)):
    in_specs = (
        P(None, "dom", "mode"),
        P("dom"),
        P(),
        P(),
        P(),
        P("dom", None, None, None),
        P("dom", None),
        P("dom"),
        P(None, "dom"),
    )
    return jax.shard_map(
        functools.partial(per_device, dims),
        mesh=mesh,
        in_specs=in_specs,
        out_specs=P("dom"),
        check_vma=False,
    )
```

```python
import functools

import jax
import jax.numpy as jnp
from jax import lax
from jax.experimental import pallas as pl
from jax.experimental.pallas import tpu as pltpu
from jax.sharding import PartitionSpec as P

MESH = pl.DeviceIdType.MESH
F32 = jnp.float32
BF16 = jnp.bfloat16
CORES = 2
FEATS = 32
RATE = 24
CHUNK = 256


def dot(a, b):
    return jnp.dot(a, b, preferred_element_type=F32)


def pieces_of(x, count):
    parts = []
    for _ in range(count):
        parts.append(x.astype(BF16).astype(F32))
        x = x - parts[-1]
    return parts


def ring_order(count):
    order = [0, count // 2]
    for k in range((count - 1) // 2, 0, -1):
        order += [k, -k]
    return order[:count]


def around(at, by, count):
    if by == 0:
        return at
    moved = at + by
    return jnp.where(moved >= count, moved - count, moved) if by > 0 else jnp.where(moved < 0, moved + count, moved)


def remote(src, dst, send, recv, device):
    return pltpu.make_async_remote_copy(
        src_ref=src,
        dst_ref=dst,
        send_sem=send,
        recv_sem=recv,
        device_id=device,
        device_id_type=MESH,
    )


def kernel(
    dims,
    shapes_h, mass_h, spec_h, freq_h, damp_h, rec_h, conn_h, cnt_h, shd_h,
    out_ref,
    shapes, mass, spec, freq, damp, rec, rec_rows, rec_line, conn, cnt, shd, codes, in_sem,
    rate_w, row_feats, col_feats, row_mat, col_mat, rows_a, corr,
    halo_out, halo_in, halo_send, halo_recv,
    lev_own, lev_x, lev_z, lx_send, lx_recv, lz_send, lz_recv,
    onehot, recov, gathered, near, reach, forces,
    far, f_send, f_pass, f_recv,
    gain_own, gains, g_send, g_recv,
    scaled, total, res_own, r_send, r_recv,
):
    nz, nx, ny = dims
    n_dom, n_mode = nz * nx, ny * CORES
    block = shapes_h.shape[2]
    half = block // 2
    nodes = shapes_h.shape[1]
    elems = conn_h.shape[1]
    slots = conn_h.shape[0]
    share = shd_h.shape[1]
    comps = forces.shape[0]
    part = comps // ny
    wide = CORES * block

    dom = lax.axis_index("dom")
    mode = lax.axis_index("mode")
    zi, yi = lax.div(dom, nx), lax.div(mode, CORES)
    xi, core = dom - zi * nx, mode - yi * CORES
    other = 1 - core
    sibling = (dom, yi * CORES + other)
    up = around(dom, 1, n_dom)
    down = around(dom, -1, n_dom)
    chips_from = [around(yi, k, ny) for k in ring_order(ny)]
    chips_to = [around(yi, -k, ny) for k in ring_order(ny)]
    x_peers = [(zi * nx + around(xi, k, nx), mode) for k in ring_order(nx)[1:]]
    z_peers = [(around(zi, k, nz) * nx + xi, mode) for k in ring_order(nz)[1:]]
    mode_peers = [(dom, chip * CORES + c) for chip in chips_to[1:] for c in range(CORES)] + [sibling]

    own = pl.multiple_of(mode * block, block)
    pairs = [
        (conn_h, conn),
        (cnt_h, cnt),
        (shd_h, shd),
        (shapes_h, shapes),
        (mass_h, mass),
        (rec_h, rec),
        (freq_h, freq),
        (damp_h, damp),
        (spec_h.at[:, pl.ds(own, block)], spec),
    ]
    loads = [pltpu.make_async_copy(a, b, in_sem.at[i]) for i, (a, b) in enumerate(pairs)]
    for load in loads[:5]:
        load.start()

    barrier = pltpu.get_barrier_semaphore()
    greeted = z_peers + mode_peers[:2] + x_peers + mode_peers[2:] + [(up, mode), (down, mode)]
    for peer in greeted:
        pl.semaphore_signal(barrier, inc=1, device_id=peer, device_id_type=MESH)
    for load in loads[5:]:
        load.start()

    for load in loads[:5]:
        load.wait()
    parts3 = pieces_of(mass[...], 3)
    row8 = lax.broadcasted_iota(jnp.int32, (8, nodes), 0)
    mass3 = jnp.zeros((8, nodes), F32)
    for i in range(3):
        mass3 = jnp.where(row8 == i, parts3[i], mass3)
    mass3 = mass3.astype(BF16)
    terms = []
    square = jnp.zeros((8, block), F32)
    for d in range(3):
        terms.append(jnp.sum(dot(mass3, shapes[d]), axis=0, keepdims=True))
        s = shapes[d].astype(F32)
        s2h, s2l = pieces_of(s * s, 2)
        square = square + dot(mass3, s2h.astype(BF16)) + dot(mass3, s2l.astype(BF16))
    terms.append(jnp.sum(square, axis=0, keepdims=True))
    stack = jnp.concatenate(terms, axis=0)
    lev_own[...] = jnp.concatenate([stack[:, :half], stack[:, half:]], axis=0)


    codes[...] = jnp.zeros_like(codes)
    codes[pl.ds(0, slots), pl.ds(0, elems)] = conn[...].astype(F32)
    codes[pl.ds(slots, 1), pl.ds(0, elems)] = cnt[...].astype(F32)
    codes[pl.ds(slots + 1, 2), pl.ds(0, share)] = shd[...].astype(F32)
    columns = jnp.transpose(codes[...])
    node_lane = lax.broadcasted_iota(jnp.int32, (share, nodes), 1).astype(F32)
    pick = jnp.concatenate(
        [
            jnp.where(columns[0:share, slots + 1 + side : slots + 2 + side] == node_lane, 1.0, 0.0)
            for side in range(2)
        ],
        axis=0,
    ).astype(BF16)
    for d in range(3):
        halo_out[d] = dot(pick, shapes[d]).astype(BF16)

    pl.semaphore_wait(barrier, len(greeted))
    x_copies = [
        remote(lev_own, lev_x.at[k], lx_send.at[k], lx_recv.at[k], peer)
        for k, peer in enumerate(x_peers)
    ]
    for copy in x_copies:
        copy.start()


    lower, upper = pl.ds(0, share), pl.ds(share, share)
    halo_copies = [
        remote(halo_out.at[:, upper], halo_in.at[:, lower], halo_send.at[0], halo_recv.at[0], (up, mode)),
        remote(halo_out.at[:, lower], halo_in.at[:, upper], halo_send.at[1], halo_recv.at[1], (down, mode)),
    ]
    for copy in halo_copies:
        copy.start()

    for load in loads[5:]:
        load.wait()
    table_lane = lax.broadcasted_iota(jnp.int32, (elems, nodes + 2 * share), 1).astype(F32)
    for s in range(slots):
        code = columns[0:elems, s : s + 1]
        live = columns[0:elems, slots : slots + 1] > s
        is_low = jnp.logical_and(code >= nodes, code < nodes + share)
        is_high = code >= nodes + share
        ground_low = jnp.where(is_low, jnp.where(dom == 0, 1.0, 0.0), 0.0)
        ground_high = jnp.where(is_high, jnp.where(dom == n_dom - 1, 1.0, 0.0), 0.0)
        kept = jnp.where(live, 1.0, 0.0) * (1.0 - ground_low) * (1.0 - ground_high)
        code = jnp.where(kept > 0.5, code, -1.0)
        onehot[pl.ds(s * elems, elems)] = jnp.where(code == table_lane, 1.0, 0.0).astype(BF16)

    per = comps // elems
    for k in range(per):
        for d in range(3):
            rec_rows[pl.ds(d * slots * per + k, slots, stride=per), pl.ds(0, elems)] = rec[k, d].astype(F32)
    for i in range(3 * slots):
        rec_line[:, pl.ds(i * elems, elems)] = rec_rows[pl.ds(i * per, per), pl.ds(0, elems)]
    rec_wide = rec_line[...]
    lane_elem = lax.broadcasted_iota(jnp.int32, rec_wide.shape, 1) % elems
    for e in range(0, elems, 2):
        recov[pl.ds(e * per, 2 * per)] = jnp.concatenate(
            [jnp.where(lane_elem == e + i, rec_wide, 0.0) for i in range(2)], axis=0
        ).astype(BF16)

    parts = slots * elems
    for d in range(3):
        gathered[pl.ds(d * parts, parts)] = dot(onehot[:, pl.ds(0, nodes)], shapes[d]).astype(BF16)
        reach[:, pl.ds(d * 2 * share, 2 * share)] = dot(
            recov[:, pl.ds(d * parts, parts)], onehot[:, pl.ds(nodes, 2 * share)]
        ).astype(BF16)
    near[...] = dot(recov[...], gathered[...])

    groups = freq.shape[0]
    w = freq[...]
    u = w * w * 0.25
    rate = damp[...] * w
    rate_w[...] = rate
    one = jnp.ones_like(w)
    uu = pieces_of(u * u, 3)
    u_h, u_m, u_l = pieces_of(u, 3)
    rr = pieces_of(rate * rate, 2)
    ru = pieces_of(rate * u, 2)
    r1 = pieces_of(rate, 2)
    left = [*uu, one, one, one, u_h, u_h, u_m, u_m, u_h, u_l]
    right = [one, one, one, *uu] + [-2.0 * v for v in (u_h, u_m, u_h, u_m, u_l, u_h)]
    for (p_h, p_m), (q_h, q_m) in ((rr, (u_h, u_m)), (ru, r1), (r1, ru), ((u_h, u_m), rr)):
        left += [p_h, p_h, p_m]
        right += [q_h, q_m, q_h]
    zero = jnp.zeros_like(w)
    left += [rate] + [zero] * (FEATS - len(left) - 1)
    right += [zero] * (FEATS - len(right))
    for feats, values in ((row_feats, left), (col_feats, right)):
        for i in range(FEATS):
            feats[pl.ds(i * groups, groups)] = values[i]
    per_chip = wide // 128
    per_core = block // 128
    for step in range(ny):
        for j in range(per_chip):
            g = chips_from[step] * per_chip + j
            at = pl.ds(step * wide + j * 128, 128)
            turned = jnp.transpose(row_feats[pl.ds(g, FEATS, stride=groups)])
            row_mat[at] = turned.astype(BF16)
            rows_a[at] = jnp.broadcast_to(turned[:, RATE : RATE + 1], (128, 128))
        for j in range(per_core):
            g = chips_from[step] * per_chip + core * per_core + j
            col_mat[:, pl.ds(step * block + j * 128, 128)] = col_feats[
                pl.ds(g, FEATS, stride=groups)
            ].astype(BF16)

    def correlate(step):
        base = step * (step + 1) // 2 * wide
        vs = [
            rate_w[pl.ds(chips_from[step] * per_chip + core * per_core + j, 1)]
            for j in range(per_core)
        ]
        cols = col_mat[:, pl.ds(step * block, block)]
        for r in range(0, (step + 1) * wide, CHUNK):
            bottom = dot(row_mat[pl.ds(r, CHUNK)], cols)
            a = rows_a[pl.ds(r, CHUNK)]
            for j in range(per_core):
                value = (a + vs[j]) * pltpu.reciprocal(bottom[:, j * 128 : (j + 1) * 128], approx=True)
                corr[pl.ds(base + r, CHUNK), pl.ds(j * 128, 128)] = value.astype(BF16)

    for step in range(0, 3):
        correlate(step)

    for copy in halo_copies:
        copy.wait_recv()
    forces[...] = (near[...] + dot(reach[...], halo_in[...].reshape(6 * share, block))).astype(BF16)

    def rows_of(chip):
        return forces.at[pl.ds(pl.multiple_of(chip * part, part), part)]

    f_copies = [None] + [
        remote(
            rows_of(chips_to[s]),
            far.at[s, core],
            f_send.at[s],
            f_recv.at[s, core],
            (dom, chips_to[s] * CORES + core),
        )
        for s in range(1, ny)
    ]
    for copy in f_copies[1:]:
        copy.start()
    f_passes = [remote(rows_of(yi), far.at[0, core], f_pass.at[0], f_recv.at[0, core], sibling)] + [
        remote(far.at[s, core], far.at[s, core], f_pass.at[s], f_recv.at[s, core], sibling)
        for s in range(1, ny)
    ]
    f_passes[0].start()
    far[0, core] = forces[pl.ds(pl.multiple_of(yi * part, part), part)]

    for copy in x_copies:
        copy.wait_recv()
    lev_sum = lev_own[...]
    for k in range(nx - 1):
        lev_sum = lev_sum + lev_x[k]
    lev_z[nz - 1] = lev_sum
    z_copies = [
        remote(lev_z.at[nz - 1], lev_z.at[k], lz_send.at[k], lz_recv.at[k], peer)
        for k, peer in enumerate(z_peers)
    ]
    for copy in z_copies:
        copy.start()

    for step in range(3, min(8, ny)):
        correlate(step)

    for copy in z_copies:
        copy.wait_recv()
    lev_all = lev_z[nz - 1]
    for k in range(nz - 1):
        lev_all = lev_all + lev_z[k]
    w2 = freq[pl.ds(mode * per_core, per_core)]
    scale2 = jnp.sqrt(0.5 * damp[pl.ds(mode * per_core, per_core)]) * (w2 * jnp.sqrt(w2))
    sp = spec[...]
    for h in range(2):
        rows = lev_all[4 * h : 4 * h + 3] / lev_all[4 * h + 3 : 4 * h + 4]
        rows = rows * sp[:, h * half : (h + 1) * half] * scale2[h : h + 1]
        gain_own[pl.ds(3 * h, 3)] = rows
    six = pl.ds(0, 6)

    g_copies = [
        remote(
            gain_own.at[six],
            gains.at[t, core, six],
            g_send.at[t, c],
            g_recv.at[t, core],
            (dom, chips_to[t] * CORES + c),
        )
        for t in range(1, ny)
        for c in range(CORES)
    ] + [remote(gain_own.at[six], gains.at[0, core, six], g_send.at[0, 0], g_recv.at[0, core], sibling)]
    for copy in g_copies:
        copy.start()
    gains[0, core, six] = gain_own[six]

    def hand_on(s):
        f_copies[s].wait_recv()
        f_passes[s].start()

    for step in range(8, ny):
        correlate(step)
    total[...] = jnp.zeros_like(total)

    def arrival(buffer, sem):
        pltpu.make_async_copy(buffer, buffer, sem).wait()

    for step in range(ny):
        for s in range(step + 2, min(step + 3, ny)) if step else range(1, min(3, ny)):
            hand_on(s)
        arrival(far.at[step, other], f_recv.at[step, other])
        for c in range(CORES) if step else ():
            arrival(gains.at[step, c, six], g_recv.at[step, c])
        if step == 0:
            arrival(gains.at[0, other, six], g_recv.at[0, other])
        for c in range(CORES):
            f = far[step, c].astype(F32)
            g = gains[step, c]
            for d in range(3):
                for h in range(2):
                    zz = f[:, h * half : (h + 1) * half] * g[3 * h + d : 3 * h + d + 1]
                    scaled[
                        pl.ds(d * part, part), pl.ds(step * wide + c * block + h * half, half)
                    ] = zz.astype(BF16)
        base = step * (step + 1) // 2 * wide
        acc = dot(scaled[:, pl.ds(step * wide, wide)], corr[pl.ds(base + step * wide, wide)])
        if step:
            acc = acc + 2.0 * dot(scaled[:, pl.ds(0, step * wide)], corr[pl.ds(base, step * wide)])
        mine = pl.ds(pl.multiple_of(step * wide + core * block, block), block)
        acc = acc * scaled[:, mine].astype(F32)
        add = acc[:, 0:128]
        for j in range(1, per_core):
            add = add + acc[:, j * 128 : (j + 1) * 128]
        total[...] += add

    summed = total[pl.ds(0, part)]
    for d in range(1, 3):
        summed = summed + total[pl.ds(d * part, part)]
    copies = 128 // part
    turned = jnp.transpose(jnp.concatenate([summed] * copies, axis=0))
    line = jnp.sum(turned, axis=0, keepdims=True)
    lane = lax.broadcasted_iota(jnp.int32, (1, 128), 1)
    res_own[...] = jnp.where(lane // part == yi - lax.div(yi, copies) * copies, line, 0.0)

    r_copies = [
        remote(res_own, out_ref.at[pl.ds(mode, 1)], r_send.at[k], r_recv.at[mode], peer)
        for k, peer in enumerate(mode_peers)
    ]
    for copy in r_copies:
        copy.start()
    keep = pltpu.make_async_copy(res_own, out_ref.at[pl.ds(mode, 1)], r_recv.at[mode])
    keep.start()
    for copy in halo_copies + x_copies + z_copies + f_copies[1:] + f_passes + g_copies:
        copy.wait_send()
    for _, m in mode_peers:
        arrival(out_ref.at[pl.ds(m, 1)], r_recv.at[m])
    keep.wait()
    for copy in r_copies:
        copy.wait_send()


def per_device(
    dims, shapes, masses, spectral, frequencies, damping, recovery, connectivity, node_count, shared
):
    nz, nx, ny = dims
    n_mode = ny * CORES
    _, nodes, block = shapes.shape
    elems, slots = connectivity.shape
    per = recovery.shape[1]
    share = shared.shape[1]
    modes = frequencies.shape[0]
    comps = elems * per
    part = comps // ny
    wide = CORES * block
    parts = slots * elems
    groups = modes // 128
    dma = pltpu.SemaphoreType.DMA
    vmem = pltpu.VMEM
    scratch = [
        vmem((3, nodes, block), BF16),
        vmem((1, nodes), F32),
        vmem((3, block), F32),
        vmem((groups, 128), F32),
        vmem((groups, 128), F32),
        vmem((per, 3, slots, elems), BF16),
        vmem((3 * slots * per, 128), F32),
        vmem((per, 3 * parts), F32),
        vmem((slots, elems), jnp.int32),
        vmem((1, elems), jnp.int32),
        vmem((2, share), jnp.int32),
        vmem((8, 128), F32),
        dma((9,)),
        vmem((groups, 128), F32),
        vmem((FEATS * groups, 128), F32),
        vmem((FEATS * groups, 128), F32),
        vmem((modes, FEATS), BF16),
        vmem((FEATS, modes // CORES), BF16),
        vmem((modes, 128), F32),
        vmem((ny * (ny + 1) // 2 * wide, block), BF16),
        vmem((3, 2 * share, block), BF16),
        vmem((3, 2 * share, block), BF16),
        dma((2,)),
        dma((2,)),
        vmem((8, block // 2), F32),
        vmem((nx - 1, 8, block // 2), F32),
        vmem((nz, 8, block // 2), F32),
        dma((nx - 1,)),
        dma((nx - 1,)),
        dma((nz - 1,)),
        dma((nz - 1,)),
        vmem((parts, nodes + 2 * share), BF16),
        vmem((comps, 3 * parts), BF16),
        vmem((3 * parts, block), BF16),
        vmem((comps, block), F32),
        vmem((comps, 6 * share), BF16),
        vmem((comps, block), BF16),
        vmem((ny, CORES, part, block), BF16),
        dma((ny,)),
        dma((ny,)),
        dma((ny, CORES)),
        vmem((8, block // 2), F32),
        vmem((ny, CORES, 8, block // 2), F32),
        dma((ny, CORES)),
        dma((ny, CORES)),
        vmem((3 * part, modes), BF16),
        vmem((3 * part, 128), F32),
        vmem((1, 128), F32),
        dma((n_mode - 1,)),
        dma((n_mode,)),
    ]
    out = pl.pallas_call(
        functools.partial(kernel, dims),
        out_shape=jax.ShapeDtypeStruct((n_mode, 128), F32),
        in_specs=[pl.BlockSpec(memory_space=pltpu.HBM)] * 9,
        out_specs=pl.BlockSpec(memory_space=pltpu.HBM),
        scratch_shapes=scratch,
        compiler_params=pltpu.CompilerParams(
            collective_id=0, has_side_effects=True, vmem_limit_bytes=56 * 1024 * 1024
        ),
    )(
        shapes,
        masses.reshape(1, nodes),
        spectral,
        frequencies.reshape(groups, 128),
        damping.reshape(groups, 128),
        recovery.transpose(1, 3, 2, 0),
        connectivity.transpose(1, 0),
        node_count.reshape(1, elems),
        shared,
    )
    return jnp.sum(out.reshape(comps // 128, n_mode * 128 // comps, 128), axis=1).reshape(comps)


def solution(mesh, dims=(4, 8, 8)):
    in_specs = (
        P(None, "dom", "mode"),
        P("dom"),
        P(),
        P(),
        P(),
        P("dom", None, None, None),
        P("dom", None),
        P("dom"),
        P(None, "dom"),
    )
    return jax.shard_map(
        functools.partial(per_device, dims),
        mesh=mesh,
        in_specs=in_specs,
        out_specs=P("dom"),
        check_vma=False,
    )
```

```python
import functools

import jax
import jax.numpy as jnp
from jax import lax
from jax.experimental import pallas as pl
from jax.experimental.pallas import tpu as pltpu
from jax.sharding import PartitionSpec as P

MESH = pl.DeviceIdType.MESH
F32 = jnp.float32
BF16 = jnp.bfloat16
CORES = 2
FEATS = 32
RATE = 24
CHUNK = 256


def dot(a, b):
    return jnp.dot(a, b, preferred_element_type=F32)


def pieces_of(x, count):
    parts = []
    for _ in range(count):
        parts.append(x.astype(BF16).astype(F32))
        x = x - parts[-1]
    return parts


def ring_order(count):
    order = [0, count // 2]
    for k in range((count - 1) // 2, 0, -1):
        order += [k, -k]
    return order[:count]


def around(at, by, count):
    if by == 0:
        return at
    moved = at + by
    return jnp.where(moved >= count, moved - count, moved) if by > 0 else jnp.where(moved < 0, moved + count, moved)


def remote(src, dst, send, recv, device):
    return pltpu.make_async_remote_copy(
        src_ref=src,
        dst_ref=dst,
        send_sem=send,
        recv_sem=recv,
        device_id=device,
        device_id_type=MESH,
    )


def kernel(
    dims,
    shapes_h, mass_h, spec_h, freq_h, damp_h, rec_h, conn_h, cnt_h, shd_h,
    out_ref,
    shapes, mass, spec, freq, damp, rec, rec_rows, rec_line, conn, cnt, shd, codes, in_sem,
    rate_w, row_feats, col_feats, row_mat, col_mat, rows_a, corr,
    halo_out, halo_in, halo_send, halo_recv,
    lev_own, lev_x, lev_z, lx_send, lx_recv, lz_send, lz_recv,
    onehot, recov, gathered, near, reach, forces,
    far, f_send, f_pass, f_recv,
    gain_own, gains, g_send, g_recv,
    scaled, total, res_own, r_send, r_recv,
):
    nz, nx, ny = dims
    n_dom, n_mode = nz * nx, ny * CORES
    block = shapes_h.shape[2]
    half = block // 2
    nodes = shapes_h.shape[1]
    elems = conn_h.shape[1]
    slots = conn_h.shape[0]
    share = shd_h.shape[1]
    comps = forces.shape[0]
    part = comps // ny
    wide = CORES * block

    dom = lax.axis_index("dom")
    mode = lax.axis_index("mode")
    zi, yi = lax.div(dom, nx), lax.div(mode, CORES)
    xi, core = dom - zi * nx, mode - yi * CORES
    other = 1 - core
    sibling = (dom, yi * CORES + other)
    up = around(dom, 1, n_dom)
    down = around(dom, -1, n_dom)
    chips_from = [around(yi, k, ny) for k in ring_order(ny)]
    chips_to = [around(yi, -k, ny) for k in ring_order(ny)]
    x_peers = [(zi * nx + around(xi, k, nx), mode) for k in ring_order(nx)[1:]]
    z_peers = [(around(zi, k, nz) * nx + xi, mode) for k in ring_order(nz)[1:]]
    mode_peers = [(dom, chip * CORES + c) for chip in chips_to[1:] for c in range(CORES)] + [sibling]

    own = pl.multiple_of(mode * block, block)
    pairs = [
        (conn_h, conn),
        (cnt_h, cnt),
        (shd_h, shd),
        (shapes_h, shapes),
        (mass_h, mass),
        (rec_h, rec),
        (freq_h, freq),
        (damp_h, damp),
        (spec_h.at[:, pl.ds(own, block)], spec),
    ]
    loads = [pltpu.make_async_copy(a, b, in_sem.at[i]) for i, (a, b) in enumerate(pairs)]
    for load in loads[:5]:
        load.start()

    barrier = pltpu.get_barrier_semaphore()
    greeted = z_peers + mode_peers[:2] + x_peers + mode_peers[2:] + [(up, mode), (down, mode)]
    for peer in greeted:
        pl.semaphore_signal(barrier, inc=1, device_id=peer, device_id_type=MESH)
    for load in loads[5:]:
        load.start()

    for load in loads[:5]:
        load.wait()
    parts3 = pieces_of(mass[...], 3)
    row8 = lax.broadcasted_iota(jnp.int32, (8, nodes), 0)
    mass3 = jnp.zeros((8, nodes), F32)
    for i in range(3):
        mass3 = jnp.where(row8 == i, parts3[i], mass3)
    mass3 = mass3.astype(BF16)
    terms = []
    square = jnp.zeros((8, block), F32)
    for d in range(3):
        terms.append(jnp.sum(dot(mass3, shapes[d]), axis=0, keepdims=True))
        s = shapes[d].astype(F32)
        s2h, s2l = pieces_of(s * s, 2)
        square = square + dot(mass3, s2h.astype(BF16)) + dot(mass3, s2l.astype(BF16))
    terms.append(jnp.sum(square, axis=0, keepdims=True))
    stack = jnp.concatenate(terms, axis=0)
    lev_own[...] = jnp.concatenate([stack[:, :half], stack[:, half:]], axis=0)


    codes[...] = jnp.zeros_like(codes)
    codes[pl.ds(0, slots), pl.ds(0, elems)] = conn[...].astype(F32)
    codes[pl.ds(slots, 1), pl.ds(0, elems)] = cnt[...].astype(F32)
    codes[pl.ds(slots + 1, 2), pl.ds(0, share)] = shd[...].astype(F32)
    columns = jnp.transpose(codes[...])
    node_lane = lax.broadcasted_iota(jnp.int32, (share, nodes), 1).astype(F32)
    pick = jnp.concatenate(
        [
            jnp.where(columns[0:share, slots + 1 + side : slots + 2 + side] == node_lane, 1.0, 0.0)
            for side in range(2)
        ],
        axis=0,
    ).astype(BF16)
    for d in range(3):
        halo_out[d] = dot(pick, shapes[d]).astype(BF16)

    pl.semaphore_wait(barrier, len(greeted))
    lower, upper = pl.ds(0, share), pl.ds(share, share)
    halo_copies = [
        remote(halo_out.at[:, upper], halo_in.at[:, lower], halo_send.at[0], halo_recv.at[0], (up, mode)),
        remote(halo_out.at[:, lower], halo_in.at[:, upper], halo_send.at[1], halo_recv.at[1], (down, mode)),
    ]
    for copy in halo_copies:
        copy.start()
    x_copies = [
        remote(lev_own, lev_x.at[k], lx_send.at[k], lx_recv.at[k], peer)
        for k, peer in enumerate(x_peers)
    ]
    for copy in x_copies:
        copy.start()


    for load in loads[5:]:
        load.wait()
    table_lane = lax.broadcasted_iota(jnp.int32, (elems, nodes + 2 * share), 1).astype(F32)
    for s in range(slots):
        code = columns[0:elems, s : s + 1]
        live = columns[0:elems, slots : slots + 1] > s
        is_low = jnp.logical_and(code >= nodes, code < nodes + share)
        is_high = code >= nodes + share
        ground_low = jnp.where(is_low, jnp.where(dom == 0, 1.0, 0.0), 0.0)
        ground_high = jnp.where(is_high, jnp.where(dom == n_dom - 1, 1.0, 0.0), 0.0)
        kept = jnp.where(live, 1.0, 0.0) * (1.0 - ground_low) * (1.0 - ground_high)
        code = jnp.where(kept > 0.5, code, -1.0)
        onehot[pl.ds(s * elems, elems)] = jnp.where(code == table_lane, 1.0, 0.0).astype(BF16)

    per = comps // elems
    for k in range(per):
        for d in range(3):
            rec_rows[pl.ds(d * slots * per + k, slots, stride=per), pl.ds(0, elems)] = rec[k, d].astype(F32)
    for i in range(3 * slots):
        rec_line[:, pl.ds(i * elems, elems)] = rec_rows[pl.ds(i * per, per), pl.ds(0, elems)]
    rec_wide = rec_line[...]
    lane_elem = lax.broadcasted_iota(jnp.int32, rec_wide.shape, 1) % elems
    for e in range(0, elems, 2):
        recov[pl.ds(e * per, 2 * per)] = jnp.concatenate(
            [jnp.where(lane_elem == e + i, rec_wide, 0.0) for i in range(2)], axis=0
        ).astype(BF16)

    parts = slots * elems
    for d in range(3):
        gathered[pl.ds(d * parts, parts)] = dot(onehot[:, pl.ds(0, nodes)], shapes[d]).astype(BF16)
        reach[:, pl.ds(d * 2 * share, 2 * share)] = dot(
            recov[:, pl.ds(d * parts, parts)], onehot[:, pl.ds(nodes, 2 * share)]
        ).astype(BF16)
    near[...] = dot(recov[...], gathered[...])

    groups = freq.shape[0]
    w = freq[...]
    u = w * w * 0.25
    rate = damp[...] * w
    rate_w[...] = rate
    one = jnp.ones_like(w)
    uu = pieces_of(u * u, 3)
    u_h, u_m, u_l = pieces_of(u, 3)
    rr = pieces_of(rate * rate, 2)
    ru = pieces_of(rate * u, 2)
    r1 = pieces_of(rate, 2)
    left = [*uu, one, one, one, u_h, u_h, u_m, u_m, u_h, u_l]
    right = [one, one, one, *uu] + [-2.0 * v for v in (u_h, u_m, u_h, u_m, u_l, u_h)]
    for (p_h, p_m), (q_h, q_m) in ((rr, (u_h, u_m)), (ru, r1), (r1, ru), ((u_h, u_m), rr)):
        left += [p_h, p_h, p_m]
        right += [q_h, q_m, q_h]
    zero = jnp.zeros_like(w)
    left += [rate] + [zero] * (FEATS - len(left) - 1)
    right += [zero] * (FEATS - len(right))
    for feats, values in ((row_feats, left), (col_feats, right)):
        for i in range(FEATS):
            feats[pl.ds(i * groups, groups)] = values[i]
    per_chip = wide // 128
    per_core = block // 128
    for step in range(ny):
        for j in range(per_chip):
            g = chips_from[step] * per_chip + j
            at = pl.ds(step * wide + j * 128, 128)
            turned = jnp.transpose(row_feats[pl.ds(g, FEATS, stride=groups)])
            row_mat[at] = turned.astype(BF16)
            rows_a[at] = jnp.broadcast_to(turned[:, RATE : RATE + 1], (128, 128))
        for j in range(per_core):
            g = chips_from[step] * per_chip + core * per_core + j
            col_mat[:, pl.ds(step * block + j * 128, 128)] = col_feats[
                pl.ds(g, FEATS, stride=groups)
            ].astype(BF16)

    def correlate(step):
        base = step * (step + 1) // 2 * wide
        vs = [
            rate_w[pl.ds(chips_from[step] * per_chip + core * per_core + j, 1)]
            for j in range(per_core)
        ]
        cols = col_mat[:, pl.ds(step * block, block)]
        for r in range(0, (step + 1) * wide, CHUNK):
            bottom = dot(row_mat[pl.ds(r, CHUNK)], cols)
            a = rows_a[pl.ds(r, CHUNK)]
            for j in range(per_core):
                value = (a + vs[j]) * pltpu.reciprocal(bottom[:, j * 128 : (j + 1) * 128], approx=True)
                corr[pl.ds(base + r, CHUNK), pl.ds(j * 128, 128)] = value.astype(BF16)

    for step in range(0, 3):
        correlate(step)

    for copy in halo_copies:
        copy.wait_recv()
    forces[...] = (near[...] + dot(reach[...], halo_in[...].reshape(6 * share, block))).astype(BF16)

    def rows_of(chip):
        return forces.at[pl.ds(pl.multiple_of(chip * part, part), part)]

    f_copies = [None] + [
        remote(
            rows_of(chips_to[s]),
            far.at[s, core],
            f_send.at[s],
            f_recv.at[s, core],
            (dom, chips_to[s] * CORES + core),
        )
        for s in range(1, ny)
    ]
    for copy in f_copies[1:]:
        copy.start()
    f_passes = [remote(rows_of(yi), far.at[0, core], f_pass.at[0], f_recv.at[0, core], sibling)] + [
        remote(far.at[s, core], far.at[s, core], f_pass.at[s], f_recv.at[s, core], sibling)
        for s in range(1, ny)
    ]
    f_passes[0].start()
    far[0, core] = forces[pl.ds(pl.multiple_of(yi * part, part), part)]

    for copy in x_copies:
        copy.wait_recv()
    lev_sum = lev_own[...]
    for k in range(nx - 1):
        lev_sum = lev_sum + lev_x[k]
    lev_z[nz - 1] = lev_sum
    z_copies = [
        remote(lev_z.at[nz - 1], lev_z.at[k], lz_send.at[k], lz_recv.at[k], peer)
        for k, peer in enumerate(z_peers)
    ]
    for copy in z_copies:
        copy.start()

    for step in range(3, min(8, ny)):
        correlate(step)

    for copy in z_copies:
        copy.wait_recv()
    lev_all = lev_z[nz - 1]
    for k in range(nz - 1):
        lev_all = lev_all + lev_z[k]
    w2 = freq[pl.ds(mode * per_core, per_core)]
    scale2 = jnp.sqrt(0.5 * damp[pl.ds(mode * per_core, per_core)]) * (w2 * jnp.sqrt(w2))
    sp = spec[...]
    for h in range(2):
        rows = lev_all[4 * h : 4 * h + 3] / lev_all[4 * h + 3 : 4 * h + 4]
        rows = rows * sp[:, h * half : (h + 1) * half] * scale2[h : h + 1]
        gain_own[pl.ds(3 * h, 3)] = rows
    six = pl.ds(0, 6)

    g_copies = [
        remote(
            gain_own.at[six],
            gains.at[t, core, six],
            g_send.at[t, c],
            g_recv.at[t, core],
            (dom, chips_to[t] * CORES + c),
        )
        for t in range(1, ny)
        for c in range(CORES)
    ] + [remote(gain_own.at[six], gains.at[0, core, six], g_send.at[0, 0], g_recv.at[0, core], sibling)]
    for copy in g_copies:
        copy.start()
    gains[0, core, six] = gain_own[six]

    def hand_on(s):
        f_copies[s].wait_recv()
        f_passes[s].start()

    for step in range(8, ny):
        correlate(step)
    total[...] = jnp.zeros_like(total)

    def arrival(buffer, sem):
        pltpu.make_async_copy(buffer, buffer, sem).wait()

    for step in range(ny):
        for s in range(step + 2, min(step + 3, ny)) if step else range(1, min(3, ny)):
            hand_on(s)
        arrival(far.at[step, other], f_recv.at[step, other])
        for c in range(CORES) if step else ():
            arrival(gains.at[step, c, six], g_recv.at[step, c])
        if step == 0:
            arrival(gains.at[0, other, six], g_recv.at[0, other])
        for c in range(CORES):
            f = far[step, c].astype(F32)
            g = gains[step, c]
            for d in range(3):
                for h in range(2):
                    zz = f[:, h * half : (h + 1) * half] * g[3 * h + d : 3 * h + d + 1]
                    scaled[
                        pl.ds(d * part, part), pl.ds(step * wide + c * block + h * half, half)
                    ] = zz.astype(BF16)
        base = step * (step + 1) // 2 * wide
        acc = dot(scaled[:, pl.ds(step * wide, wide)], corr[pl.ds(base + step * wide, wide)])
        if step:
            acc = acc + 2.0 * dot(scaled[:, pl.ds(0, step * wide)], corr[pl.ds(base, step * wide)])
        mine = pl.ds(pl.multiple_of(step * wide + core * block, block), block)
        acc = acc * scaled[:, mine].astype(F32)
        add = acc[:, 0:128]
        for j in range(1, per_core):
            add = add + acc[:, j * 128 : (j + 1) * 128]
        total[...] += add

    summed = total[pl.ds(0, part)]
    for d in range(1, 3):
        summed = summed + total[pl.ds(d * part, part)]
    copies = 128 // part
    turned = jnp.transpose(jnp.concatenate([summed] * copies, axis=0))
    line = jnp.sum(turned, axis=0, keepdims=True)
    lane = lax.broadcasted_iota(jnp.int32, (1, 128), 1)
    res_own[...] = jnp.where(lane // part == yi - lax.div(yi, copies) * copies, line, 0.0)

    r_copies = [
        remote(res_own, out_ref.at[pl.ds(mode, 1)], r_send.at[k], r_recv.at[mode], peer)
        for k, peer in enumerate(mode_peers)
    ]
    for copy in r_copies:
        copy.start()
    keep = pltpu.make_async_copy(res_own, out_ref.at[pl.ds(mode, 1)], r_recv.at[mode])
    keep.start()
    for copy in halo_copies + x_copies + z_copies + f_copies[1:] + f_passes + g_copies:
        copy.wait_send()
    for _, m in mode_peers:
        arrival(out_ref.at[pl.ds(m, 1)], r_recv.at[m])
    keep.wait()
    for copy in r_copies:
        copy.wait_send()


def per_device(
    dims, shapes, masses, spectral, frequencies, damping, recovery, connectivity, node_count, shared
):
    nz, nx, ny = dims
    n_mode = ny * CORES
    _, nodes, block = shapes.shape
    elems, slots = connectivity.shape
    per = recovery.shape[1]
    share = shared.shape[1]
    modes = frequencies.shape[0]
    comps = elems * per
    part = comps // ny
    wide = CORES * block
    parts = slots * elems
    groups = modes // 128
    dma = pltpu.SemaphoreType.DMA
    vmem = pltpu.VMEM
    scratch = [
        vmem((3, nodes, block), BF16),
        vmem((1, nodes), F32),
        vmem((3, block), F32),
        vmem((groups, 128), F32),
        vmem((groups, 128), F32),
        vmem((per, 3, slots, elems), BF16),
        vmem((3 * slots * per, 128), F32),
        vmem((per, 3 * parts), F32),
        vmem((slots, elems), jnp.int32),
        vmem((1, elems), jnp.int32),
        vmem((2, share), jnp.int32),
        vmem((8, 128), F32),
        dma((9,)),
        vmem((groups, 128), F32),
        vmem((FEATS * groups, 128), F32),
        vmem((FEATS * groups, 128), F32),
        vmem((modes, FEATS), BF16),
        vmem((FEATS, modes // CORES), BF16),
        vmem((modes, 128), F32),
        vmem((ny * (ny + 1) // 2 * wide, block), BF16),
        vmem((3, 2 * share, block), BF16),
        vmem((3, 2 * share, block), BF16),
        dma((2,)),
        dma((2,)),
        vmem((8, block // 2), F32),
        vmem((nx - 1, 8, block // 2), F32),
        vmem((nz, 8, block // 2), F32),
        dma((nx - 1,)),
        dma((nx - 1,)),
        dma((nz - 1,)),
        dma((nz - 1,)),
        vmem((parts, nodes + 2 * share), BF16),
        vmem((comps, 3 * parts), BF16),
        vmem((3 * parts, block), BF16),
        vmem((comps, block), F32),
        vmem((comps, 6 * share), BF16),
        vmem((comps, block), BF16),
        vmem((ny, CORES, part, block), BF16),
        dma((ny,)),
        dma((ny,)),
        dma((ny, CORES)),
        vmem((8, block // 2), F32),
        vmem((ny, CORES, 8, block // 2), F32),
        dma((ny, CORES)),
        dma((ny, CORES)),
        vmem((3 * part, modes), BF16),
        vmem((3 * part, 128), F32),
        vmem((1, 128), F32),
        dma((n_mode - 1,)),
        dma((n_mode,)),
    ]
    out = pl.pallas_call(
        functools.partial(kernel, dims),
        out_shape=jax.ShapeDtypeStruct((n_mode, 128), F32),
        in_specs=[pl.BlockSpec(memory_space=pltpu.HBM)] * 9,
        out_specs=pl.BlockSpec(memory_space=pltpu.HBM),
        scratch_shapes=scratch,
        compiler_params=pltpu.CompilerParams(
            collective_id=0, has_side_effects=True, vmem_limit_bytes=56 * 1024 * 1024
        ),
    )(
        shapes,
        masses.reshape(1, nodes),
        spectral,
        frequencies.reshape(groups, 128),
        damping.reshape(groups, 128),
        recovery.transpose(1, 3, 2, 0),
        connectivity.transpose(1, 0),
        node_count.reshape(1, elems),
        shared,
    )
    return jnp.sum(out.reshape(comps // 128, n_mode * 128 // comps, 128), axis=1).reshape(comps)


def solution(mesh, dims=(4, 8, 8)):
    in_specs = (
        P(None, "dom", "mode"),
        P("dom"),
        P(),
        P(),
        P(),
        P("dom", None, None, None),
        P("dom", None),
        P("dom"),
        P(None, "dom"),
    )
    return jax.shard_map(
        functools.partial(per_device, dims),
        mesh=mesh,
        in_specs=in_specs,
        out_specs=P("dom"),
        check_vma=False,
    )
```

```python
import functools

import jax
import jax.numpy as jnp
from jax import lax
from jax.experimental import pallas as pl
from jax.experimental.pallas import tpu as pltpu
from jax.sharding import PartitionSpec as P

MESH = pl.DeviceIdType.MESH
F32 = jnp.float32
BF16 = jnp.bfloat16
CORES = 2
FEATS = 32
RATE = 24
CHUNK = 256


def dot(a, b):
    return jnp.dot(a, b, preferred_element_type=F32)


def pieces_of(x, count):
    parts = []
    for _ in range(count):
        parts.append(x.astype(BF16).astype(F32))
        x = x - parts[-1]
    return parts


def ring_order(count):
    order = [0, count // 2]
    for k in range((count - 1) // 2, 0, -1):
        order += [k, -k]
    return order[:count]


def around(at, by, count):
    if by == 0:
        return at
    moved = at + by
    return jnp.where(moved >= count, moved - count, moved) if by > 0 else jnp.where(moved < 0, moved + count, moved)


def remote(src, dst, send, recv, device):
    return pltpu.make_async_remote_copy(
        src_ref=src,
        dst_ref=dst,
        send_sem=send,
        recv_sem=recv,
        device_id=device,
        device_id_type=MESH,
    )


def kernel(
    dims,
    shapes_h, mass_h, spec_h, freq_h, damp_h, rec_h, conn_h, cnt_h, shd_h,
    out_ref,
    shapes, mass, spec, freq, damp, rec, rec_rows, rec_line, conn, cnt, shd, codes, in_sem,
    rate_w, row_feats, col_feats, row_mat, col_mat, rows_a, corr,
    halo_out, halo_in, halo_send, halo_recv,
    lev_own, lev_x, lev_z, lx_send, lx_recv, lz_send, lz_recv,
    onehot, recov, gathered, near, reach, forces,
    far, f_send, f_pass, f_recv,
    gain_own, gains, g_send, g_recv,
    scaled, total, res_own, r_send, r_recv,
):
    nz, nx, ny = dims
    n_dom, n_mode = nz * nx, ny * CORES
    block = shapes_h.shape[2]
    half = block // 2
    nodes = shapes_h.shape[1]
    elems = conn_h.shape[1]
    slots = conn_h.shape[0]
    share = shd_h.shape[1]
    comps = forces.shape[0]
    part = comps // ny
    wide = CORES * block

    dom = lax.axis_index("dom")
    mode = lax.axis_index("mode")
    zi, yi = lax.div(dom, nx), lax.div(mode, CORES)
    xi, core = dom - zi * nx, mode - yi * CORES
    other = 1 - core
    sibling = (dom, yi * CORES + other)
    up = around(dom, 1, n_dom)
    down = around(dom, -1, n_dom)
    chips_from = [around(yi, k, ny) for k in ring_order(ny)]
    chips_to = [around(yi, -k, ny) for k in ring_order(ny)]
    x_peers = [(zi * nx + around(xi, k, nx), mode) for k in ring_order(nx)[1:]]
    z_peers = [(around(zi, k, nz) * nx + xi, mode) for k in ring_order(nz)[1:]]
    mode_peers = [(dom, chip * CORES + c) for chip in chips_to[1:] for c in range(CORES)] + [sibling]

    own = pl.multiple_of(mode * block, block)
    pairs = [
        (conn_h, conn),
        (cnt_h, cnt),
        (shd_h, shd),
        (shapes_h, shapes),
        (mass_h, mass),
        (rec_h, rec),
        (freq_h, freq),
        (damp_h, damp),
        (spec_h.at[:, pl.ds(own, block)], spec),
    ]
    loads = [pltpu.make_async_copy(a, b, in_sem.at[i]) for i, (a, b) in enumerate(pairs)]
    for load in loads[:5]:
        load.start()

    barrier = pltpu.get_barrier_semaphore()
    greeted = z_peers + mode_peers[:2] + x_peers + mode_peers[2:] + [(up, mode), (down, mode)]
    for peer in greeted:
        pl.semaphore_signal(barrier, inc=1, device_id=peer, device_id_type=MESH)
    for load in loads[5:]:
        load.start()

    for load in loads[:5]:
        load.wait()
    parts3 = pieces_of(mass[...], 3)
    row8 = lax.broadcasted_iota(jnp.int32, (8, nodes), 0)
    mass3 = jnp.zeros((8, nodes), F32)
    for i in range(3):
        mass3 = jnp.where(row8 == i, parts3[i], mass3)
    mass3 = mass3.astype(BF16)
    terms = []
    square = jnp.zeros((8, block), F32)
    for d in range(3):
        terms.append(jnp.sum(dot(mass3, shapes[d]), axis=0, keepdims=True))
        s = shapes[d].astype(F32)
        s2h, s2l = pieces_of(s * s, 2)
        square = square + dot(mass3, s2h.astype(BF16)) + dot(mass3, s2l.astype(BF16))
    terms.append(jnp.sum(square, axis=0, keepdims=True))
    stack = jnp.concatenate(terms, axis=0)
    lev_own[...] = jnp.concatenate([stack[:, :half], stack[:, half:]], axis=0)


    codes[...] = jnp.zeros_like(codes)
    codes[pl.ds(0, slots), pl.ds(0, elems)] = conn[...].astype(F32)
    codes[pl.ds(slots, 1), pl.ds(0, elems)] = cnt[...].astype(F32)
    codes[pl.ds(slots + 1, 2), pl.ds(0, share)] = shd[...].astype(F32)
    columns = jnp.transpose(codes[...])
    node_lane = lax.broadcasted_iota(jnp.int32, (share, nodes), 1).astype(F32)
    pick = jnp.concatenate(
        [
            jnp.where(columns[0:share, slots + 1 + side : slots + 2 + side] == node_lane, 1.0, 0.0)
            for side in range(2)
        ],
        axis=0,
    ).astype(BF16)
    for d in range(3):
        halo_out[d] = dot(pick, shapes[d]).astype(BF16)

    pl.semaphore_wait(barrier, len(greeted))
    x_copies = [
        remote(lev_own, lev_x.at[k], lx_send.at[k], lx_recv.at[k], peer)
        for k, peer in enumerate(x_peers)
    ]
    for copy in x_copies:
        copy.start()


    lower, upper = pl.ds(0, share), pl.ds(share, share)
    halo_copies = [
        remote(halo_out.at[:, upper], halo_in.at[:, lower], halo_send.at[0], halo_recv.at[0], (up, mode)),
        remote(halo_out.at[:, lower], halo_in.at[:, upper], halo_send.at[1], halo_recv.at[1], (down, mode)),
    ]
    for copy in halo_copies:
        copy.start()

    for load in loads[5:]:
        load.wait()
    table_lane = lax.broadcasted_iota(jnp.int32, (elems, nodes + 2 * share), 1).astype(F32)
    for s in range(slots):
        code = columns[0:elems, s : s + 1]
        live = columns[0:elems, slots : slots + 1] > s
        is_low = jnp.logical_and(code >= nodes, code < nodes + share)
        is_high = code >= nodes + share
        ground_low = jnp.where(is_low, jnp.where(dom == 0, 1.0, 0.0), 0.0)
        ground_high = jnp.where(is_high, jnp.where(dom == n_dom - 1, 1.0, 0.0), 0.0)
        kept = jnp.where(live, 1.0, 0.0) * (1.0 - ground_low) * (1.0 - ground_high)
        code = jnp.where(kept > 0.5, code, -1.0)
        onehot[pl.ds(s * elems, elems)] = jnp.where(code == table_lane, 1.0, 0.0).astype(BF16)

    per = comps // elems
    for k in range(per):
        for d in range(3):
            rec_rows[pl.ds(d * slots * per + k, slots, stride=per), pl.ds(0, elems)] = rec[k, d].astype(F32)
    for i in range(3 * slots):
        rec_line[:, pl.ds(i * elems, elems)] = rec_rows[pl.ds(i * per, per), pl.ds(0, elems)]
    rec_wide = rec_line[...]
    lane_elem = lax.broadcasted_iota(jnp.int32, rec_wide.shape, 1) % elems
    for e in range(0, elems, 2):
        recov[pl.ds(e * per, 2 * per)] = jnp.concatenate(
            [jnp.where(lane_elem == e + i, rec_wide, 0.0) for i in range(2)], axis=0
        ).astype(BF16)

    parts = slots * elems
    for d in range(3):
        gathered[pl.ds(d * parts, parts)] = dot(onehot[:, pl.ds(0, nodes)], shapes[d]).astype(BF16)
        reach[:, pl.ds(d * 2 * share, 2 * share)] = dot(
            recov[:, pl.ds(d * parts, parts)], onehot[:, pl.ds(nodes, 2 * share)]
        ).astype(BF16)
    near[...] = dot(recov[...], gathered[...])

    groups = freq.shape[0]
    w = freq[...]
    u = w * w * 0.25
    rate = damp[...] * w
    rate_w[...] = rate
    one = jnp.ones_like(w)
    uu = pieces_of(u * u, 3)
    u_h, u_m, u_l = pieces_of(u, 3)
    rr = pieces_of(rate * rate, 2)
    ru = pieces_of(rate * u, 2)
    r1 = pieces_of(rate, 2)
    left = [*uu, one, one, one, u_h, u_h, u_m, u_m, u_h, u_l]
    right = [one, one, one, *uu] + [-2.0 * v for v in (u_h, u_m, u_h, u_m, u_l, u_h)]
    for (p_h, p_m), (q_h, q_m) in ((rr, (u_h, u_m)), (ru, r1), (r1, ru), ((u_h, u_m), rr)):
        left += [p_h, p_h, p_m]
        right += [q_h, q_m, q_h]
    zero = jnp.zeros_like(w)
    left += [rate] + [zero] * (FEATS - len(left) - 1)
    right += [zero] * (FEATS - len(right))
    for feats, values in ((row_feats, left), (col_feats, right)):
        for i in range(FEATS):
            feats[pl.ds(i * groups, groups)] = values[i]
    per_chip = wide // 128
    per_core = block // 128
    for step in range(ny):
        for j in range(per_chip):
            g = chips_from[step] * per_chip + j
            at = pl.ds(step * wide + j * 128, 128)
            turned = jnp.transpose(row_feats[pl.ds(g, FEATS, stride=groups)])
            row_mat[at] = turned.astype(BF16)
            rows_a[at] = jnp.broadcast_to(turned[:, RATE : RATE + 1], (128, 128))
        for j in range(per_core):
            g = chips_from[step] * per_chip + core * per_core + j
            col_mat[:, pl.ds(step * block + j * 128, 128)] = col_feats[
                pl.ds(g, FEATS, stride=groups)
            ].astype(BF16)

    def correlate(step):
        base = step * (step + 1) // 2 * wide
        vs = [
            rate_w[pl.ds(chips_from[step] * per_chip + core * per_core + j, 1)]
            for j in range(per_core)
        ]
        cols = col_mat[:, pl.ds(step * block, block)]
        for r in range(0, (step + 1) * wide, CHUNK):
            bottom = dot(row_mat[pl.ds(r, CHUNK)], cols)
            a = rows_a[pl.ds(r, CHUNK)]
            for j in range(per_core):
                value = (a + vs[j]) * pltpu.reciprocal(bottom[:, j * 128 : (j + 1) * 128], approx=True)
                corr[pl.ds(base + r, CHUNK), pl.ds(j * 128, 128)] = value.astype(BF16)

    for step in range(0, 3):
        correlate(step)

    for copy in halo_copies:
        copy.wait_recv()
    forces[...] = (near[...] + dot(reach[...], halo_in[...].reshape(6 * share, block))).astype(BF16)

    def rows_of(chip):
        return forces.at[pl.ds(pl.multiple_of(chip * part, part), part)]

    f_copies = [None] + [
        remote(
            rows_of(chips_to[s]),
            far.at[s, core],
            f_send.at[s],
            f_recv.at[s, core],
            (dom, chips_to[s] * CORES + core),
        )
        for s in range(1, ny)
    ]
    for copy in f_copies[1:]:
        copy.start()
    f_passes = [remote(rows_of(yi), far.at[0, core], f_pass.at[0], f_recv.at[0, core], sibling)] + [
        remote(far.at[s, core], far.at[s, core], f_pass.at[s], f_recv.at[s, core], sibling)
        for s in range(1, ny)
    ]
    f_passes[0].start()
    far[0, core] = forces[pl.ds(pl.multiple_of(yi * part, part), part)]

    for copy in x_copies:
        copy.wait_recv()
    lev_sum = lev_own[...]
    for k in range(nx - 1):
        lev_sum = lev_sum + lev_x[k]
    lev_z[nz - 1] = lev_sum
    z_copies = [
        remote(lev_z.at[nz - 1], lev_z.at[k], lz_send.at[k], lz_recv.at[k], peer)
        for k, peer in enumerate(z_peers)
    ]
    for copy in z_copies:
        copy.start()

    for step in range(3, min(8, ny)):
        correlate(step)

    for copy in z_copies:
        copy.wait_recv()
    lev_all = lev_z[nz - 1]
    for k in range(nz - 1):
        lev_all = lev_all + lev_z[k]
    w2 = freq[pl.ds(mode * per_core, per_core)]
    scale2 = jnp.sqrt(0.5 * damp[pl.ds(mode * per_core, per_core)]) * (w2 * jnp.sqrt(w2))
    sp = spec[...]
    for h in range(2):
        rows = lev_all[4 * h : 4 * h + 3] / lev_all[4 * h + 3 : 4 * h + 4]
        rows = rows * sp[:, h * half : (h + 1) * half] * scale2[h : h + 1]
        gain_own[pl.ds(3 * h, 3)] = rows
    six = pl.ds(0, 6)

    g_copies = [
        remote(
            gain_own.at[six],
            gains.at[t, core, six],
            g_send.at[t, c],
            g_recv.at[t, core],
            (dom, chips_to[t] * CORES + c),
        )
        for t in range(1, ny)
        for c in range(CORES)
    ] + [remote(gain_own.at[six], gains.at[0, core, six], g_send.at[0, 0], g_recv.at[0, core], sibling)]
    for copy in g_copies:
        copy.start()
    gains[0, core, six] = gain_own[six]

    def hand_on(s):
        f_copies[s].wait_recv()
        f_passes[s].start()

    for step in range(8, ny):
        correlate(step)
    for s in range(1, ny):
        hand_on(s)
    total[...] = jnp.zeros_like(total)

    def arrival(buffer, sem):
        pltpu.make_async_copy(buffer, buffer, sem).wait()

    for step in range(ny):
        arrival(far.at[step, other], f_recv.at[step, other])
        for c in range(CORES) if step else ():
            arrival(gains.at[step, c, six], g_recv.at[step, c])
        if step == 0:
            arrival(gains.at[0, other, six], g_recv.at[0, other])
        for c in range(CORES):
            f = far[step, c].astype(F32)
            g = gains[step, c]
            for d in range(3):
                for h in range(2):
                    zz = f[:, h * half : (h + 1) * half] * g[3 * h + d : 3 * h + d + 1]
                    scaled[
                        pl.ds(d * part, part), pl.ds(step * wide + c * block + h * half, half)
                    ] = zz.astype(BF16)
        base = step * (step + 1) // 2 * wide
        acc = dot(scaled[:, pl.ds(step * wide, wide)], corr[pl.ds(base + step * wide, wide)])
        if step:
            acc = acc + 2.0 * dot(scaled[:, pl.ds(0, step * wide)], corr[pl.ds(base, step * wide)])
        mine = pl.ds(pl.multiple_of(step * wide + core * block, block), block)
        acc = acc * scaled[:, mine].astype(F32)
        add = acc[:, 0:128]
        for j in range(1, per_core):
            add = add + acc[:, j * 128 : (j + 1) * 128]
        total[...] += add

    summed = total[pl.ds(0, part)]
    for d in range(1, 3):
        summed = summed + total[pl.ds(d * part, part)]
    copies = 128 // part
    turned = jnp.transpose(jnp.concatenate([summed] * copies, axis=0))
    line = jnp.sum(turned, axis=0, keepdims=True)
    lane = lax.broadcasted_iota(jnp.int32, (1, 128), 1)
    res_own[...] = jnp.where(lane // part == yi - lax.div(yi, copies) * copies, line, 0.0)

    r_copies = [
        remote(res_own, out_ref.at[pl.ds(mode, 1)], r_send.at[k], r_recv.at[mode], peer)
        for k, peer in enumerate(mode_peers)
    ]
    for copy in r_copies:
        copy.start()
    keep = pltpu.make_async_copy(res_own, out_ref.at[pl.ds(mode, 1)], r_recv.at[mode])
    keep.start()
    for copy in halo_copies + x_copies + z_copies + f_copies[1:] + f_passes + g_copies:
        copy.wait_send()
    for _, m in mode_peers:
        arrival(out_ref.at[pl.ds(m, 1)], r_recv.at[m])
    keep.wait()
    for copy in r_copies:
        copy.wait_send()


def per_device(
    dims, shapes, masses, spectral, frequencies, damping, recovery, connectivity, node_count, shared
):
    nz, nx, ny = dims
    n_mode = ny * CORES
    _, nodes, block = shapes.shape
    elems, slots = connectivity.shape
    per = recovery.shape[1]
    share = shared.shape[1]
    modes = frequencies.shape[0]
    comps = elems * per
    part = comps // ny
    wide = CORES * block
    parts = slots * elems
    groups = modes // 128
    dma = pltpu.SemaphoreType.DMA
    vmem = pltpu.VMEM
    scratch = [
        vmem((3, nodes, block), BF16),
        vmem((1, nodes), F32),
        vmem((3, block), F32),
        vmem((groups, 128), F32),
        vmem((groups, 128), F32),
        vmem((per, 3, slots, elems), BF16),
        vmem((3 * slots * per, 128), F32),
        vmem((per, 3 * parts), F32),
        vmem((slots, elems), jnp.int32),
        vmem((1, elems), jnp.int32),
        vmem((2, share), jnp.int32),
        vmem((8, 128), F32),
        dma((9,)),
        vmem((groups, 128), F32),
        vmem((FEATS * groups, 128), F32),
        vmem((FEATS * groups, 128), F32),
        vmem((modes, FEATS), BF16),
        vmem((FEATS, modes // CORES), BF16),
        vmem((modes, 128), F32),
        vmem((ny * (ny + 1) // 2 * wide, block), BF16),
        vmem((3, 2 * share, block), BF16),
        vmem((3, 2 * share, block), BF16),
        dma((2,)),
        dma((2,)),
        vmem((8, block // 2), F32),
        vmem((nx - 1, 8, block // 2), F32),
        vmem((nz, 8, block // 2), F32),
        dma((nx - 1,)),
        dma((nx - 1,)),
        dma((nz - 1,)),
        dma((nz - 1,)),
        vmem((parts, nodes + 2 * share), BF16),
        vmem((comps, 3 * parts), BF16),
        vmem((3 * parts, block), BF16),
        vmem((comps, block), F32),
        vmem((comps, 6 * share), BF16),
        vmem((comps, block), BF16),
        vmem((ny, CORES, part, block), BF16),
        dma((ny,)),
        dma((ny,)),
        dma((ny, CORES)),
        vmem((8, block // 2), F32),
        vmem((ny, CORES, 8, block // 2), F32),
        dma((ny, CORES)),
        dma((ny, CORES)),
        vmem((3 * part, modes), BF16),
        vmem((3 * part, 128), F32),
        vmem((1, 128), F32),
        dma((n_mode - 1,)),
        dma((n_mode,)),
    ]
    out = pl.pallas_call(
        functools.partial(kernel, dims),
        out_shape=jax.ShapeDtypeStruct((n_mode, 128), F32),
        in_specs=[pl.BlockSpec(memory_space=pltpu.HBM)] * 9,
        out_specs=pl.BlockSpec(memory_space=pltpu.HBM),
        scratch_shapes=scratch,
        compiler_params=pltpu.CompilerParams(
            collective_id=0, has_side_effects=True, vmem_limit_bytes=56 * 1024 * 1024
        ),
    )(
        shapes,
        masses.reshape(1, nodes),
        spectral,
        frequencies.reshape(groups, 128),
        damping.reshape(groups, 128),
        recovery.transpose(1, 3, 2, 0),
        connectivity.transpose(1, 0),
        node_count.reshape(1, elems),
        shared,
    )
    return jnp.sum(out.reshape(comps // 128, n_mode * 128 // comps, 128), axis=1).reshape(comps)


def solution(mesh, dims=(4, 8, 8)):
    in_specs = (
        P(None, "dom", "mode"),
        P("dom"),
        P(),
        P(),
        P(),
        P("dom", None, None, None),
        P("dom", None),
        P("dom"),
        P(None, "dom"),
    )
    return jax.shard_map(
        functools.partial(per_device, dims),
        mesh=mesh,
        in_specs=in_specs,
        out_specs=P("dom"),
        check_vma=False,
    )
```
